256 devices in a mesh: tok: 16 (over y, x), voc: 8 (over z), hid: 2 (over core).
Axes of the slice: x: 4, y: 4, z: 8, core: 2. Of those that a mesh axis runs over, the one named last changes fastest.
Arguments:
- hidden: bfloat16 [2048, 4096], P('tok', 'hid')
- head_weight: bfloat16 [16000, 4096], P(('tok', 'voc'), 'hid')
- target_logits: bfloat16 [2048, 128256], P('tok', ('voc', 'hid'))
- vocab_order: int32 [128256], P(('voc', 'hid')), may hold values from 0 to 128255, as said below
- draft_map: int32 [16000], replicated, may hold values from 0 to 128255, as said below
- token_weight: float32 [2048], P('tok'), may hold values from 4 to 40
Outputs:
- token_kl: float32 [2048], P(('tok', 'hid'))
- grad_hidden: bfloat16 [2048, 4096], P(('tok', 'voc'), 'hid')
- grad_weight: bfloat16 [16000, 4096], P(('tok', 'voc'), 'hid')
The draws below stay inside these ranges and needn't reach their ends.
Inputs may be any that keep to these rules, and one draw needn't show every extreme that they name: A permutation of the target ids: storage column j of target_logits holds the logit of target id vocab_order[j]. `draft_map`: 16000 distinct target ids. Draft id k belongs to voc index (k // 125) % 8. Among the 8016 storage columns of any one device of voc+hid, at most 250 hold the target ids of draft ids that belong to one voc index, and in every draw some device holds exactly 250 for some voc index.
All inputs are finite; a program needn't handle non-finite values.
Results may differ from the reference program's by a relative error of at most 0.018.
Values may be sent and summed in bfloat16 or wider, within the bound.
A program may use at most 64 MiB of HBM per device.

```python
import math
import jax
import jax.numpy as jnp
from jax import lax

D = 4096
VD = 16000
VT = 128256
TOKENS = 2048
VD_DEV = 2000
BLK = 125
VOCAB_SHARDS = 16
VT_DEV = 8016
CAP = 250
N_VOC = 8


def head_matrix(key):
    return 3.0 * jax.random.normal(jax.random.fold_in(key, 11), (VD, D), jnp.float32) / math.sqrt(D)


def routing_tables(key):
    key = jax.random.fold_in(key, 500)
    subkeys = jax.random.split(key, 6)
    random_noise = jax.random.randint(subkeys[0], (N_VOC, VOCAB_SHARDS, CAP), 0, 4096)
    offset = jax.random.randint(subkeys[5], (), 0, VOCAB_SHARDS)
    usage_frequency = 4096 * (VOCAB_SHARDS - (jnp.arange(VOCAB_SHARDS) + offset) % VOCAB_SHARDS) // VOCAB_SHARDS
    pinned_entries = jax.random.randint(subkeys[1], (N_VOC,), 0, VOCAB_SHARDS)
    extra_reward = jnp.where(jnp.arange(VOCAB_SHARDS)[None, :] == pinned_entries[:, None], 1 << 20, 0)
    ranking_value = random_noise + usage_frequency[None, :, None] + extra_reward[:, :, None]
    ranking = jnp.argsort(-ranking_value.reshape(N_VOC, VOCAB_SHARDS * CAP), axis=1, stable=True)[:, :VD_DEV]
    shard_of = ranking // CAP
    slot_of = ranking % CAP
    positions = jax.vmap(lambda subkey: jax.random.permutation(subkey, VT_DEV))(jax.random.split(subkeys[2], VOCAB_SHARDS))
    owner_rows = jnp.arange(N_VOC)[:, None]
    storage = shard_of * VT_DEV + positions[shard_of, owner_rows * CAP + slot_of]
    shuffle = jax.vmap(lambda subkey: jax.random.permutation(subkey, VD_DEV))(jax.random.split(subkeys[3], N_VOC))
    storage = jnp.take_along_axis(storage, shuffle, axis=1)
    vocab_order = jax.random.permutation(subkeys[4], VT).astype(jnp.int32)
    draft_ids = vocab_order[storage]
    draft_map = draft_ids.reshape(N_VOC, VD_DEV // BLK, BLK).transpose(1, 0, 2).reshape(VD)
    return (vocab_order, draft_map.astype(jnp.int32))


def draw_vocab_order(key, part):
    tables = routing_tables(key)
    return tables[0]


def draw_draft_map(key, part):
    tables = routing_tables(key)
    return tables[1]


def draw_head_weight(key, part):
    weight = head_matrix(key)
    return weight.astype(jnp.bfloat16)


def draw_hidden(key, part):
    key = jax.random.fold_in(key, 2)
    subkeys = jax.random.split(key, 1)
    activity = jax.random.normal(subkeys[0], (TOKENS, D), jnp.float32)
    return activity.astype(jnp.bfloat16)


def draw_target_logits(key, part):
    key = jax.random.fold_in(key, 3)
    subkeys = jax.random.split(key, 3)
    row_scale = jnp.exp(jax.random.uniform(subkeys[0], (TOKENS, 1), jnp.float32, 0.0, math.log(math.sqrt(10.0))))
    col_scale = jnp.exp(jax.random.uniform(subkeys[1], (1, VT), jnp.float32, 0.0, math.log(math.sqrt(10.0))))
    values = 1.5 * row_scale * col_scale * jax.random.normal(subkeys[2], (TOKENS, VT), jnp.float32)
    return values.astype(jnp.bfloat16)


def shard_levels(stream_key, extent, pieces, smallest, largest):
    def one(position, shards_of):
        steps = jax.random.uniform(jax.random.fold_in(jax.random.fold_in(stream_key, 6), position), (shards_of,), jnp.float32, smallest / len(pieces), largest / len(pieces))
        return jnp.repeat(jnp.exp(steps), extent[position] // shards_of).reshape((-1,) + (1,) * (len(extent) - position - 1))

    loudness = one(*pieces[0])
    for cut in pieces[1:]:
        loudness = loudness * one(*cut)
    return loudness


def setup_inputs(seed: int = 0) -> dict:
    arg_keys = jax.random.split(jax.random.key(seed), 7)
    return {
        "hidden": draw_hidden(jax.random.fold_in(arg_keys[6], 71), 0),
        "head_weight": draw_head_weight(jax.random.fold_in(arg_keys[6], 71), 0),
        "target_logits": draw_target_logits(jax.random.fold_in(arg_keys[6], 71), 0),
        "vocab_order": draw_vocab_order(jax.random.fold_in(arg_keys[6], 71), 0),
        "draft_map": draw_draft_map(jax.random.fold_in(arg_keys[6], 71), 0),
        "token_weight": jnp.clip(jnp.exp(math.log(40.0) - 2.3025851 * jax.random.uniform(arg_keys[5], (TOKENS,), jnp.float32) ** shard_levels(arg_keys[5], (TOKENS,), ((0, 16),), -0.2, 0.2)), 4.0, 40.0),
    }


def reference(hidden, head_weight, target_logits, vocab_order, draft_map, token_weight):
    stored_location = jnp.zeros((VT,), jnp.int32).at[vocab_order].set(jnp.arange(VT, dtype=jnp.int32))
    column_of = stored_location[draft_map].astype(jnp.int32)
    target = jnp.take(target_logits, column_of, axis=1).astype(jnp.float32)
    weight_f = head_weight.astype(jnp.float32)
    hidden_f = hidden.astype(jnp.float32)
    draft = jnp.dot(hidden_f, weight_f.T, precision=lax.Precision.HIGHEST)
    top_target = jnp.max(target, axis=1, keepdims=True)
    target_exp = jnp.exp(target - top_target)
    target_total = jnp.sum(target_exp, axis=1)
    target_norm = top_target[:, 0] + jnp.log(target_total)
    top_draft = jnp.max(draft, axis=1, keepdims=True)
    draft_norm = top_draft[:, 0] + jnp.log(jnp.sum(jnp.exp(draft - top_draft), axis=1))
    cross_term = jnp.sum(target_exp * (target - draft), axis=1)
    token_kl = cross_term / target_total - target_norm + draft_norm
    probs = jnp.exp(target - target_norm[:, None])
    grad_logit = (token_weight[:, None] * (jnp.exp(draft - draft_norm[:, None]) - probs)).astype(jnp.bfloat16)
    grad_f = grad_logit.astype(jnp.float32)
    grad_hidden = jnp.dot(grad_f, weight_f, precision=lax.Precision.HIGHEST).astype(jnp.bfloat16)
    grad_weight = jnp.dot(grad_f.T, hidden_f, precision=lax.Precision.HIGHEST).astype(jnp.bfloat16)
    return token_kl, grad_hidden, grad_weight
```

```python
import jax
import jax.numpy as jnp
from jax import lax
from jax.experimental import pallas as pl
from jax.experimental.pallas import tpu as pltpu
from jax.sharding import PartitionSpec as P

F32, BF16, I32 = jnp.float32, jnp.bfloat16, jnp.int32
MESH = pl.DeviceIdType.MESH
NT = (((1,), (1,)), ((), ()))
COLS = 8016
BLK = 125
D2 = 2048
HALF = 1024
Z_ORDER = (4, 3, 5, 2, 6, 1, 7, 0)
STEP = 256


def iota(shape, dim):
    return lax.broadcasted_iota(I32, shape, dim)


def low_lanes(shape):
    return iota(shape, 1) < 64


def swap(a):
    return pltpu.roll(a, 64, 1)


def kernel(
    ids_ref, order_ref, logits_ref, hidden_ref, weight_ref, row_weight_ref,
    kl_ref, gh_ref, gw_ref,
    logits, loc, slot, locz, slot_send, slot_recv, src_v, src_s, logits_t, picked, pick_send, pick_recv,
    idx_v, idx_s, rows, placed, x_send, x_recv, target, hid_all, w_all, d_own, d_send, d_recv,
    stat_x, stat_z, grad, grad_t, xs, ys, x_mid, y_mid, x_fin, y_fin, z_send, z_recv,
    loc_sem, ag_s, ag_r, copy_sem, si_s, si_r, pk_s, pk_r, xa_s, xa_r, dd, sx_s, sx_r, sz_s, sz_r, gg,
    rx_s, rx_r, ry_s, ry_r, rz_s, rz_r,
):
    tok, z, c = lax.axis_index("tok"), lax.axis_index("voc"), lax.axis_index("hid")
    y, x = tok // 4, tok % 4
    shard = z * 2 + c

    def x_peer(d):
        return (y * 4 + (x + d) % 4, z, c)

    def y_peer(d):
        return ((y + d) % 4 * 4 + x, z, c)

    def tok_peer(d):
        return ((tok + d) % 16, z, c)

    def voc_peer(dz, dc):
        return (tok, (z + dz) % 8, (c + dc) % 2)

    def send(src, dst, ssem, rsem, peer):
        copy = pltpu.make_async_remote_copy(
            src_ref=src, dst_ref=dst, send_sem=ssem, recv_sem=rsem, device_id=peer, device_id_type=MESH
        )
        copy.start()
        return copy

    voc_pairs = [(dz, dc) for dz in Z_ORDER for dc in (0, 1) if dz or dc]

    barrier = pltpu.get_barrier_semaphore()
    for d in range(1, 16):
        pl.semaphore_signal(barrier, inc=1, device_id=tok_peer(d), device_id_type=MESH)
    for dz, dc in voc_pairs:
        pl.semaphore_signal(barrier, inc=1, device_id=voc_peer(dz, dc), device_id_type=MESH)

    logits_in = pltpu.make_async_copy(logits_ref, logits, copy_sem.at[0])
    hidden_in = pltpu.make_async_copy(hidden_ref, hid_all.at[:, x], copy_sem.at[1])
    weight_in = pltpu.make_async_copy(weight_ref, w_all.at[y], copy_sem.at[2])
    for copy in (logits_in, hidden_in, weight_in):
        copy.start()

    def join(zz, _):
        wanted = ids_ref[pl.ds(pl.multiple_of(zz * 128, 128), 128), :]

        def step(b, acc):
            return jnp.where(order_ref[pl.ds(b, 1), :] == wanted, b, acc)

        acc = lax.fori_loop(0, 63, step, jnp.full((128, 128), -1, I32), unroll=9)
        found = jnp.where(acc >= 0, acc * 128 + iota((128, 128), 1), -1).astype(F32)
        loc[tok, pl.ds(zz, 1), :] = jnp.max(found.T, axis=0, keepdims=True).astype(I32)
        return 0

    lax.fori_loop(0, 8, join, 0)

    pl.semaphore_wait(barrier, 30)
    loc_copies = [
        send(loc.at[tok], loc.at[tok], loc_sem.at[0, d], loc_sem.at[1, d], tok_peer(d)) for d in range(1, 16)
    ]

    def spread(source, first, peer, base):
        copies = []
        for k, (h, d) in enumerate(((0, 1), (1, -1), (1, 1), (0, -1))):
            copies.append(send(source.at[h], first(h, 0), ag_s.at[base + k], ag_r.at[base + k], peer(d)))
        return copies

    def hid_at(h, d):
        return hid_all.at[h, (x + d) % 4]

    def w_at(h, d):
        return w_all.at[(y + d) % 4, h]

    hid_copies = spread(hidden_ref, hid_at, x_peer, 0)
    w_copies = spread(weight_ref, w_at, y_peer, 6)

    logits_in.wait()
    eye = (iota((128, 128), 0) == iota((128, 128), 1)).astype(BF16)

    def turn(b, _):
        start = pl.multiple_of(b * 128, 128)
        block = logits[:, pl.ds(start, 128)]
        logits_t[pl.ds(start, 128), :] = lax.dot_general(eye, block, NT, preferred_element_type=F32)
        return 0

    lax.fori_loop(0, COLS // 128, turn, 0, unroll=2)
    tail = COLS - COLS % 128
    logits_t[tail:, :] = lax.dot_general(
        eye[: COLS % 128, : COLS % 128], logits[:, tail:], NT, preferred_element_type=F32
    )

    for copy in loc_copies:
        copy.wait()

    r0, r1 = iota((128, 128), 0), iota((128, 128), 1)
    order = ((r0 >> 4 == (r1 & 7)) & ((r0 & 15) == r1 >> 3)).astype(BF16)
    before = (r0 < r1).astype(BF16)
    earlier = ((r0 >> 4 == r1 >> 4) & ((r1 & 15) < (r0 & 15))).astype(BF16)
    where_all = loc[...].reshape(128, 128)
    high = jnp.dot(order, (where_all >> 6).astype(F32).astype(BF16), preferred_element_type=F32)
    low = jnp.dot(order, (where_all & 63).astype(F32).astype(BF16), preferred_element_type=F32)
    place = high * 64.0 + low
    held = place >= 0.0
    held_b = held.astype(F32).astype(BF16)
    in_row = jnp.dot(held_b, before, preferred_element_type=F32)
    count = jnp.dot(held_b, jnp.ones((128, 128), BF16), preferred_element_type=F32)
    rank = in_row + jnp.dot(earlier, count.astype(BF16), preferred_element_type=F32)
    slots = jnp.where(held, rank, -1.0)
    slot[...] = slots
    locz[...] = place
    slot_send[...] = slots.astype(BF16).reshape(8, 16, 128)
    slot_copies = [
        send(
            slot_send.at[(z + dz) % 8], slot_recv.at[shard],
            si_s.at[dz * 2 + dc], si_r.at[dz * 2 + dc], voc_peer(dz, dc),
        )
        for dz, dc in voc_pairs
    ]
    slot_recv[shard] = slot_send[z]

    for zz in range(8):
        for half in range(2):
            mine = (iota((128, 128), 0) + half * 128).astype(F32)

            def step(t, acc, zz=zz, mine=mine):
                row = pl.ds(zz * 16 + t, 1)
                return jnp.where(slot[row, :] == mine, locz[row, :], acc)

            acc = lax.fori_loop(0, 16, step, jnp.zeros((128, 128), F32), unroll=4)
            column = jnp.sum(acc.T, axis=0, keepdims=True).astype(I32)
            src_v[zz : zz + 1, half * 128 : half * 128 + 128] = jnp.clip(column, 0, COLS - 1)

    to_smem = pltpu.make_async_copy(src_v, src_s, copy_sem.at[3])
    to_smem.start()
    to_smem.wait()

    hidden_in.wait()
    weight_in.wait()

    def pass_on(copies, at, peer, base):
        out = []
        for k, d in ((0, -1), (1, 1)):
            copies[k].wait_recv()
            out.append(send(at(k, d), at(k, d), ag_s.at[base + 4 + k], ag_r.at[base + 4 + k], peer(-d)))
        return out

    hid_more = pass_on(hid_copies, hid_at, x_peer, 0)
    w_more = pass_on(w_copies, w_at, y_peer, 6)

    lanes = low_lanes((128, 128))
    pick_copies = []
    for dz in Z_ORDER:
        zz = (z + dz) % 8

        def pick(g, _, zz=zz):
            for k in range(16):
                s = g * 16 + k
                picked[zz, pl.ds(s, 1), :] = logits_t[pl.ds(src_s[zz, s], 1), :]
            return 0

        lax.fori_loop(0, 16, pick, 0)
        first, second = picked[zz, :128, :], picked[zz, 128:, :]
        pick_send[zz, 0] = jnp.where(lanes, first, swap(second)).astype(BF16)
        pick_send[zz, 1] = jnp.where(lanes, swap(first), second).astype(BF16)
        for dc in (0, 1):
            if dz or dc:
                pick_copies.append(
                    send(
                        pick_send.at[zz, (c + dc) % 2], pick_recv.at[shard],
                        pk_s.at[dz * 2 + dc], pk_r.at[dz * 2 + dc], voc_peer(dz, dc),
                    )
                )
    pick_recv[shard] = pick_send[z, c]

    for copy in slot_copies:
        copy.wait()
    index = jnp.zeros((16, 128), F32)
    for s in range(16):
        got = slot_recv[s].astype(F32)
        index = jnp.where(got >= 0.0, got + s * 256.0, index)
    idx_v[...] = jnp.clip(index.astype(I32), 0, 4095)
    to_smem = pltpu.make_async_copy(idx_v, idx_s, copy_sem.at[4])
    to_smem.start()
    to_smem.wait()

    for copy in hid_copies[2:] + w_copies[2:] + hid_more + w_more:
        copy.wait_recv()

    def partial_draft(core, out):
        tokens = hid_all[core].reshape(256, D2)

        def step(i, _):
            part = w_all[pl.ds(i * 2, 2)].reshape(256, D2)
            out[pl.ds(pl.multiple_of(i * 256, 256), 256), :] = lax.dot_general(
                part, tokens, NT, preferred_element_type=F32
            )
            return 0

        lax.fori_loop(0, 2, step, 0)

    partial_draft(1 - c, d_send)
    d_copy = send(d_send, d_recv, dd.at[0], dd.at[1], voc_peer(0, 1))
    partial_draft(c, d_own)

    for copy in pick_copies:
        copy.wait()

    def unpack(s, _):
        block = pick_recv[s].astype(F32)
        rows[pl.ds(pl.multiple_of(s * 256, 256), 128), :] = block
        rows[pl.ds(pl.multiple_of(s * 256 + 128, 128), 128), :] = swap(block)
        return 0

    lax.fori_loop(0, 16, unpack, 0)

    def place_rows(t, _):
        def some(g, _):
            for k in range(16):
                r = g * 16 + k
                placed[t, pl.ds(r, 1), :] = rows[pl.ds(idx_s[t, r], 1), :]
            return 0

        return lax.fori_loop(0, 8, some, 0)

    lax.fori_loop(0, 16, place_rows, 0)

    x_copies = []
    for d in (2, 1, 3, 0):
        xx = (x + d) % 4
        for k in range(2):
            x_send[xx, k * 128 : k * 128 + 128, :] = jnp.where(
                lanes, placed[k * 4 + xx], swap(placed[k * 4 + 8 + xx])
            ).astype(BF16)
        if d:
            x_copies.append(send(x_send.at[xx], x_recv.at[x], xa_s.at[d], xa_r.at[d], x_peer(d)))
    x_recv[x] = x_send[x]

    d_copy.wait()
    d_own[...] += d_recv[...]
    for copy in x_copies:
        copy.wait()
    lanes2 = low_lanes((256, 128))
    for j in range(2):
        first, second = x_recv[2 * j].astype(F32), x_recv[2 * j + 1].astype(F32)
        target[:256, j * 128 : j * 128 + 128] = jnp.where(lanes2, first, swap(second))
        target[256:, j * 128 : j * 128 + 128] = jnp.where(lanes2, swap(first), second)

    real = (iota((512, 256), 0) & 127) < BLK
    draft_l, target_l = d_own[...], target[...]
    top_d = jnp.max(jnp.where(real, draft_l, -jnp.inf), axis=0, keepdims=True)
    top_t = jnp.max(jnp.where(real, target_l, -jnp.inf), axis=0, keepdims=True)
    sum_d = jnp.sum(jnp.where(real, jnp.exp(draft_l - top_d), 0.0), axis=0, keepdims=True)
    exp_t = jnp.where(real, jnp.exp(target_l - top_t), 0.0)
    sum_t = jnp.sum(exp_t, axis=0, keepdims=True)
    cross = jnp.sum(jnp.where(real, exp_t * (target_l - draft_l), 0.0), axis=0, keepdims=True)

    def packed(stats):
        return jnp.concatenate(list(stats) + [jnp.zeros((8 - len(stats), 256), F32)], axis=0)

    def merge(ref, n):
        part = [ref[i] for i in range(n)]
        top_d, top_t = part[0][0:1], part[0][2:3]
        for p in part[1:]:
            top_d, top_t = jnp.maximum(top_d, p[0:1]), jnp.maximum(top_t, p[2:3])
        sum_d = sum(p[1:2] * jnp.exp(p[0:1] - top_d) for p in part)
        scale = [jnp.exp(p[2:3] - top_t) for p in part]
        sum_t = sum(p[3:4] * s for p, s in zip(part, scale))
        cross = sum(p[4:5] * s for p, s in zip(part, scale))
        return top_d, sum_d, top_t, sum_t, cross

    stat_x[x] = packed((top_d, sum_d, top_t, sum_t, cross, row_weight_ref[...]))
    copies = [send(stat_x.at[x], stat_x.at[x], sx_s.at[d], sx_r.at[d], x_peer(d)) for d in (2, 1, 3)]
    for copy in copies:
        copy.wait()
    row_weight = stat_x[0][5:6] + stat_x[1][5:6] + stat_x[2][5:6] + stat_x[3][5:6]
    stat_z[z] = packed(merge(stat_x, 4))
    copies = [
        send(stat_z.at[z], stat_z.at[z], sz_s.at[d], sz_r.at[d], voc_peer(d, 0)) for d in Z_ORDER[:-1]
    ]
    for copy in copies:
        copy.wait()
    top_d, sum_d, top_t, sum_t, cross = merge(stat_z, 8)
    norm_d = top_d + jnp.log(sum_d)
    norm_t = top_t + jnp.log(sum_t)
    kl_ref[...] = cross / sum_t - norm_t + norm_d

    grad_l = row_weight * (jnp.exp(d_own[...] - norm_d) - jnp.exp(target[...] - norm_t))
    grad_l = jnp.where(real, grad_l, 0.0)
    grad[c] = grad_l.astype(BF16)
    g_copy = send(grad.at[c], grad.at[c], gg.at[0], gg.at[1], voc_peer(0, 1))
    grad_t[c] = grad_l.T.astype(BF16).reshape(4, 64, 512)
    g_copy.wait()
    grad_t[1 - c] = grad[1 - c].astype(F32).T.astype(BF16).reshape(4, 64, 512)

    def hidden_half(h):
        left = grad_t[...].reshape(512, 512)

        def step(j, _):
            col = pl.multiple_of(j * STEP, STEP)
            right = w_all[:, :, :, pl.ds(h * HALF + col, STEP)].reshape(512, STEP)
            out = jnp.dot(left, right, preferred_element_type=F32).astype(BF16).reshape(2, 4, 64, STEP)
            for a in range(2):
                for b in range(4):
                    xs[h, b, a * 64 : a * 64 + 64, pl.ds(col, STEP)] = out[a, b]
            return 0

        lax.fori_loop(0, HALF // STEP, step, 0)

    def weight_half(h):
        left0, left1 = grad[0], grad[1]

        def step(j, _):
            col = pl.multiple_of(j * STEP, STEP)
            right = hid_all[:, :, :, pl.ds(h * HALF + col, STEP)].reshape(2, 256, STEP)
            out = jnp.dot(left0, right[0], preferred_element_type=F32)
            out += jnp.dot(left1, right[1], preferred_element_type=F32)
            ys[h, :, :, pl.ds(col, STEP)] = out.astype(BF16).reshape(4, 128, STEP)
            return 0

        lax.fori_loop(0, HALF // STEP, step, 0)

    def early(h, buf, mid, fin, me, peer, ss, rr):
        d = 1 - 2 * h
        return [
            send(buf.at[h, (me + 2) % 4], mid.at[h], ss.at[h], rr.at[h], peer(d)),
            send(buf.at[h, (me - d) % 4], fin.at[1 - h, h], ss.at[2 + h], rr.at[2 + h], peer(-d)),
        ]

    def late(h, first, buf, mid, fin, me, peer, ss, rr):
        d = 1 - 2 * h
        first.wait()
        block = (me + d) % 4
        buf[h, block] = (buf[h, block].astype(F32) + mid[h].astype(F32)).astype(BF16)
        return send(buf.at[h, block], fin.at[h, h], ss.at[4 + h], rr.at[4 + h], peer(d))

    x_args = (xs, x_mid, x_fin, x, x_peer, rx_s, rx_r)
    y_args = (ys, y_mid, y_fin, y, y_peer, ry_s, ry_r)
    hidden_half(0)
    x0 = early(0, *x_args)
    weight_half(0)
    y0 = early(0, *y_args)
    hidden_half(1)
    x1 = early(1, *x_args)
    weight_half(1)
    y1 = early(1, *y_args)
    x2 = [late(0, x0[0], *x_args), late(1, x1[0], *x_args)]
    y2 = [late(0, y0[0], *y_args), late(1, y1[0], *y_args)]

    def total(h, buf, fin, me):
        return buf[h, me].astype(F32) + fin[0, h].astype(F32) + fin[1, h].astype(F32)

    for copy in [x0[1], x1[1]] + x2:
        copy.wait()
    for h in range(2):
        z_send[:, :, h * HALF : h * HALF + HALF] = total(h, xs, x_fin, x).astype(BF16).reshape(8, 16, HALF)
    z_copies = [
        send(z_send.at[(z + d) % 8], z_recv.at[z], rz_s.at[d], rz_r.at[d], voc_peer(d, 0)) for d in Z_ORDER[:-1]
    ]
    for copy in [y0[1], y1[1]] + y2:
        copy.wait()
    for h in range(2):
        gw_ref[:, h * HALF : h * HALF + HALF] = total(h, ys, y_fin, y).astype(BF16)
    for copy in z_copies:
        copy.wait()
    z_recv[z] = z_send[z]
    out = z_recv[0].astype(F32)
    for i in range(1, 8):
        out += z_recv[i].astype(F32)
    gh_ref[...] = out.astype(BF16)

    for copy in hid_copies + w_copies + hid_more + w_more:
        copy.wait_send()


def body(hidden, head_weight, target_logits, vocab_order, draft_map, token_weight):
    tok, c = lax.axis_index("tok"), lax.axis_index("hid")
    ids = lax.dynamic_slice_in_dim(draft_map, tok * 8 * BLK, 8 * BLK, 0).reshape(8, BLK)
    ids = jnp.pad(ids, ((0, 0), (0, 128 - BLK)), constant_values=-2).reshape(1024, 1)
    ids = jnp.broadcast_to(ids, (1024, 128))
    order = jnp.pad(vocab_order, (0, 63 * 128 - COLS), constant_values=-1).reshape(63, 128)
    weight = jnp.pad(head_weight, ((0, 128 - BLK), (0, 0))).reshape(2, 64, D2)
    mine = lax.dynamic_slice_in_dim(token_weight, c * 64, 64, 0)
    row_weight = lax.dynamic_update_slice(jnp.zeros((256,), F32), mine, (tok % 4 * 64,)).reshape(1, 256)

    vmem = pl.BlockSpec(memory_space=pltpu.VMEM)
    hbm = pl.BlockSpec(memory_space=pl.ANY)
    dma = pltpu.SemaphoreType.DMA
    scratch = [
        pltpu.VMEM((128, COLS), BF16),
        pltpu.VMEM((16, 8, 128), I32),
        pltpu.VMEM((128, 128), F32),
        pltpu.VMEM((128, 128), F32),
        pltpu.VMEM((8, 16, 128), BF16),
        pltpu.VMEM((16, 16, 128), BF16),
        pltpu.VMEM((8, 256), I32),
        pltpu.SMEM((8, 256), I32),
        pltpu.VMEM((COLS, 128), F32),
        pltpu.VMEM((8, 256, 128), F32),
        pltpu.VMEM((8, 2, 128, 128), BF16),
        pltpu.VMEM((16, 128, 128), BF16),
        pltpu.VMEM((16, 128), I32),
        pltpu.SMEM((16, 128), I32),
        pltpu.VMEM((4096, 128), F32),
        pltpu.VMEM((16, 128, 128), F32),
        pltpu.VMEM((4, 256, 128), BF16),
        pltpu.VMEM((4, 256, 128), BF16),
        pltpu.VMEM((512, 256), F32),
        pltpu.VMEM((2, 4, 64, D2), BF16),
        pltpu.VMEM((4, 2, 64, D2), BF16),
        pltpu.VMEM((512, 256), F32),
        pltpu.VMEM((512, 256), F32),
        pltpu.VMEM((512, 256), F32),
        pltpu.VMEM((4, 8, 256), F32),
        pltpu.VMEM((8, 8, 256), F32),
        pltpu.VMEM((2, 512, 256), BF16),
        pltpu.VMEM((2, 4, 64, 512), BF16),
        pltpu.VMEM((2, 4, 128, HALF), BF16),
        pltpu.VMEM((2, 4, 128, HALF), BF16),
        pltpu.VMEM((2, 128, HALF), BF16),
        pltpu.VMEM((2, 128, HALF), BF16),
        pltpu.VMEM((2, 2, 128, HALF), BF16),
        pltpu.VMEM((2, 2, 128, HALF), BF16),
        pltpu.VMEM((8, 16, D2), BF16),
        pltpu.VMEM((8, 16, D2), BF16),
        dma((2, 16)),
        dma((12,)), dma((12,)),
        dma((5,)),
        dma((16,)), dma((16,)),
        dma((16,)), dma((16,)),
        dma((4,)), dma((4,)),
        dma((2,)),
        dma((4,)), dma((4,)),
        dma((8,)), dma((8,)),
        dma((2,)),
        dma((6,)), dma((6,)),
        dma((6,)), dma((6,)),
        dma((8,)), dma((8,)),
    ]
    kl, grad_hidden, grad_weight = pl.pallas_call(
        kernel,
        out_shape=(
            jax.ShapeDtypeStruct((1, 256), F32),
            jax.ShapeDtypeStruct((16, D2), BF16),
            jax.ShapeDtypeStruct((128, D2), BF16),
        ),
        in_specs=[vmem, vmem, hbm, hbm, hbm, vmem],
        out_specs=(vmem, vmem, vmem),
        scratch_shapes=scratch,
        compiler_params=pltpu.CompilerParams(
            collective_id=0, has_side_effects=True, vmem_limit_bytes=48 * 1024 * 1024
        ),
        name="draft_head",
    )(ids, order, target_logits, hidden.reshape(2, 64, D2), weight, row_weight)
    kl = lax.dynamic_slice_in_dim(kl.reshape(256), tok % 4 * 64, 64, 0)
    return kl, grad_hidden, grad_weight[:BLK]


def solution(mesh):
    placed = (
        P("tok", "hid"),
        P(("tok", "voc"), "hid"),
        P("tok", ("voc", "hid")),
        P(("voc", "hid")),
        P(),
        P("tok"),
    )
    return jax.shard_map(
        body,
        mesh=mesh,
        in_specs=placed,
        out_specs=(P(("tok", "hid")), P(("tok", "voc"), "hid"), P(("tok", "voc"), "hid")),
        check_vma=False,
    )
```

```python
import jax
import jax.numpy as jnp
from jax import lax
from jax.experimental import pallas as pl
from jax.experimental.pallas import tpu as pltpu
from jax.sharding import PartitionSpec as P

F32, BF16, I32 = jnp.float32, jnp.bfloat16, jnp.int32
MESH = pl.DeviceIdType.MESH
NT = (((1,), (1,)), ((), ()))
COLS = 8016
BLK = 125
D2 = 2048
Z_ORDER = (4, 3, 5, 2, 6, 1, 7, 0)
STEP = 256
PAIRS = D2 // STEP // 2
VMEM_LIMIT = 48 * 1024 * 1024


def iota(shape, dim):
    return lax.broadcasted_iota(I32, shape, dim)


def low_lanes(shape):
    return iota(shape, 1) < 64


def swap(a):
    return pltpu.roll(a, 64, 1)


def kernel(
    ids_ref, order_ref, logits_ref, hidden_ref, weight_ref, row_weight_ref,
    kl_ref, gh_ref, gw_ref,
    row_weight_own, weight, logits, loc, slot, locz, slot_send, slot_recv, src_v, src_s, logits_t, picked, pick_send, pick_recv,
    idx_v, idx_s, rows, placed, x_send, x_recv, target, hid_all, w_all, d_own, d_send, d_recv,
    stat_x, stat_z, grad, grad_t, xs, ys, x_mid, y_mid, x_fin, y_fin, z_send, z_recv,
    loc_sem, ag_s, ag_r, copy_sem, src_sem, si_s, si_r, pk_s, pk_r, xa_s, xa_r, dd, sx_s, sx_r, sz_s, sz_r, gg,
    rx_s, rx_r, ry_s, ry_r, rz_s, rz_r,
):
    tok, z, c = lax.axis_index("tok"), lax.axis_index("voc"), lax.axis_index("hid")
    y, x = tok // 4, tok % 4
    shard = z * 2 + c

    def x_peer(d):
        return (y * 4 + (x + d) % 4, z, c)

    def y_peer(d):
        return ((y + d) % 4 * 4 + x, z, c)

    def tok_peer(d):
        return ((tok + d) % 16, z, c)

    def voc_peer(dz, dc):
        return (tok, (z + dz) % 8, (c + dc) % 2)

    unsent, unreceived = [], []

    def send(src, dst, ssem, rsem, peer):
        copy = pltpu.make_async_remote_copy(
            src_ref=src, dst_ref=dst, send_sem=ssem, recv_sem=rsem, device_id=peer, device_id_type=MESH
        )
        copy.start()
        unsent.append(copy)
        unreceived.append(copy)
        return copy

    def arrive(copies):
        for copy in copies:
            copy.wait_recv()
            unreceived[:] = [other for other in unreceived if other is not copy]

    def drain():
        arrive(list(unreceived))
        for copy in unsent:
            copy.wait_send()

    voc_pairs = [(dz, dc) for dz in Z_ORDER for dc in (0, 1) if dz or dc]

    barrier = pltpu.get_barrier_semaphore()
    for d in range(1, 16):
        pl.semaphore_signal(barrier, inc=1, device_id=tok_peer(d), device_id_type=MESH)
    for dz, dc in voc_pairs:
        pl.semaphore_signal(barrier, inc=1, device_id=voc_peer(dz, dc), device_id_type=MESH)

    logits_in = pltpu.make_async_copy(logits_ref, logits, copy_sem.at[0])
    hidden_in = pltpu.make_async_copy(hidden_ref, hid_all.at[:, x], copy_sem.at[1])
    weight_in = pltpu.make_async_copy(weight_ref, weight, copy_sem.at[2])
    row_weight_in = pltpu.make_async_copy(row_weight_ref, row_weight_own, copy_sem.at[3])
    for copy in (weight_in, hidden_in, logits_in, row_weight_in):
        copy.start()

    def join(zz, _):
        wanted = jnp.broadcast_to(ids_ref[pl.ds(zz, 1), :], (128, 128)).T

        def step(b, acc):
            return jnp.where(order_ref[pl.ds(b, 1), :] == wanted, b, acc)

        acc = lax.fori_loop(0, 63, step, jnp.full((128, 128), -1, I32), unroll=9)
        found = jnp.where(acc >= 0, acc * 128 + iota((128, 128), 1), -1).astype(F32)
        loc[tok, pl.ds(zz, 1), :] = jnp.max(found.T, axis=0, keepdims=True).astype(I32)
        return 0

    lax.fori_loop(0, 8, join, 0)

    pl.semaphore_wait(barrier, 30)
    loc_copies = [
        send(loc.at[tok], loc.at[tok], loc_sem.at[0, d], loc_sem.at[1, d], tok_peer(d)) for d in range(1, 16)
    ]

    weight_in.wait()
    w_all[y, 0] = weight[:64, :]
    w_all[y, 1] = jnp.concatenate([weight[64:, :], jnp.zeros((128 - BLK, D2), BF16)], axis=0)

    def spread(source, first, peer, base):
        copies = []
        for k, (h, d) in enumerate(((0, 1), (1, -1), (1, 1), (0, -1))):
            copies.append(send(source.at[h], first(h, 0), ag_s.at[base + k], ag_r.at[base + k], peer(d)))
        return copies

    def hid_at(h, d):
        return hid_all.at[h, (x + d) % 4]

    def w_at(h, d):
        return w_all.at[(y + d) % 4, h]

    hid_copies = spread(hidden_ref, hid_at, x_peer, 0)
    w_copies = spread(w_all.at[y], w_at, y_peer, 6)

    logits_in.wait()

    def widen(b, _):
        part = pl.ds(pl.multiple_of(b * 48, 48), 48)
        logits_t[part, :] = logits[part, :].astype(F32)
        return 0

    lax.fori_loop(0, COLS // 48, widen, 0, unroll=4)

    arrive(loc_copies)

    r0, r1 = iota((128, 128), 0), iota((128, 128), 1)
    order = ((r0 >> 4 == (r1 & 7)) & ((r0 & 15) == r1 >> 3)).astype(BF16)
    before = (r0 < r1).astype(BF16)
    earlier = ((r0 >> 4 == r1 >> 4) & ((r1 & 15) < (r0 & 15))).astype(BF16)
    where_all = loc[...].reshape(128, 128)
    high = jnp.dot(order, (where_all >> 6).astype(F32).astype(BF16), preferred_element_type=F32)
    low = jnp.dot(order, (where_all & 63).astype(F32).astype(BF16), preferred_element_type=F32)
    place = high * 64.0 + low
    held = place >= 0.0
    held_b = held.astype(F32).astype(BF16)
    in_row = jnp.dot(held_b, before, preferred_element_type=F32)
    count = jnp.dot(held_b, jnp.ones((128, 128), BF16), preferred_element_type=F32)
    rank = in_row + jnp.dot(earlier, count.astype(BF16), preferred_element_type=F32)
    slots = jnp.where(held, rank, -1.0)
    slot[...] = slots
    locz[...] = place
    slot_send[...] = slots.astype(BF16).reshape(8, 16, 128)
    slot_copies = [
        send(
            slot_send.at[(z + dz) % 8], slot_recv.at[shard],
            si_s.at[dz * 2 + dc], si_r.at[dz * 2 + dc], voc_peer(dz, dc),
        )
        for dz, dc in voc_pairs
    ]
    slot_recv[shard] = slot_send[z]

    def list_slots(k):
        zz = (z + Z_ORDER[k]) % 8
        columns = []
        for half in range(2):
            mine = (iota((128, 128), 0) + half * 128).astype(F32)

            def step(t, acc, mine=mine):
                row = pl.ds(zz * 16 + t, 1)
                return jnp.where(slot[row, :] == mine, locz[row, :], acc)

            acc = lax.fori_loop(0, 16, step, jnp.zeros((128, 128), F32), unroll=8)
            columns.append(jnp.sum(acc.T, axis=0, keepdims=True))
        column = jnp.clip(jnp.concatenate(columns, axis=1).astype(I32), 0, COLS - 1)
        src_v[k] = jnp.broadcast_to(column, (8, 256))
        copy = pltpu.make_async_copy(src_v.at[k], src_s.at[k], src_sem.at[k])
        copy.start()
        return copy

    listed = list_slots(0)

    hidden_in.wait()

    def pass_on(copies, at, peer, base):
        out = []
        for k, d in ((0, -1), (1, 1)):
            arrive([copies[k]])
            out.append(send(at(k, d), at(k, d), ag_s.at[base + 4 + k], ag_r.at[base + 4 + k], peer(-d)))
        return out

    hid_more = pass_on(hid_copies, hid_at, x_peer, 0)
    w_more = pass_on(w_copies, w_at, y_peer, 6)

    lanes = low_lanes((128, 128))
    pick_copies = []
    for k, dz in enumerate(Z_ORDER):
        zz = (z + dz) % 8
        following = list_slots(k + 1) if k < 7 else None
        listed.wait()
        listed = following

        def pick(g, _, zz=zz, k=k):
            for i in range(16):
                s = g * 16 + i
                picked[zz, pl.ds(s, 1), :] = logits_t[pl.ds(src_s[k, 0, s], 1), :]
            return 0

        lax.fori_loop(0, 16, pick, 0)
        first, second = picked[zz, :128, :], picked[zz, 128:, :]
        pick_send[zz, 0] = jnp.where(lanes, first, swap(second)).astype(BF16)
        pick_send[zz, 1] = jnp.where(lanes, swap(first), second).astype(BF16)
        for dc in (0, 1):
            if dz or dc:
                pick_copies.append(
                    send(
                        pick_send.at[zz, (c + dc) % 2], pick_recv.at[shard],
                        pk_s.at[dz * 2 + dc], pk_r.at[dz * 2 + dc], voc_peer(dz, dc),
                    )
                )
    pick_recv[shard] = pick_send[z, c]

    arrive(slot_copies)
    index = jnp.zeros((16, 128), F32)
    for s in range(16):
        got = slot_recv[s].astype(F32)
        index = jnp.where(got >= 0.0, got + s * 256.0, index)
    idx_v[...] = jnp.clip(index.astype(I32), 0, 4095)
    to_smem = pltpu.make_async_copy(idx_v, idx_s, copy_sem.at[4])
    to_smem.start()
    to_smem.wait()

    arrive(hid_copies[2:] + w_copies[2:] + hid_more + w_more)

    def partial_draft(core, out):
        tokens = hid_all[core].reshape(256, D2)

        def step(i, _):
            part = w_all[pl.ds(i * 2, 2)].reshape(256, D2)
            out[pl.ds(pl.multiple_of(i * 256, 256), 256), :] = lax.dot_general(
                part, tokens, NT, preferred_element_type=F32
            )
            return 0

        lax.fori_loop(0, 2, step, 0)

    partial_draft(1 - c, d_send)
    d_copy = send(d_send, d_recv, dd.at[0], dd.at[1], voc_peer(0, 1))
    partial_draft(c, d_own)

    arrive(pick_copies)

    def unpack(s, _):
        block = pick_recv[s].astype(F32)
        rows[pl.ds(pl.multiple_of(s * 256, 256), 128), :] = block
        rows[pl.ds(pl.multiple_of(s * 256 + 128, 128), 128), :] = swap(block)
        return 0

    lax.fori_loop(0, 16, unpack, 0)

    x_copies = []
    for d in (2, 1, 3, 0):
        xx = (x + d) % 4

        def place_rows(i, _, xx=xx):
            t = (i >> 3) * 4 + xx
            for k in range(16):
                r = (i & 7) * 16 + k
                placed[t, pl.ds(r, 1), :] = rows[pl.ds(idx_s[t, r], 1), :]
            return 0

        lax.fori_loop(0, 32, place_rows, 0)
        for k in range(2):
            x_send[xx, k * 128 : k * 128 + 128, :] = jnp.where(
                lanes, placed[k * 4 + xx], swap(placed[k * 4 + 8 + xx])
            ).astype(BF16)
        if d:
            x_copies.append(send(x_send.at[xx], x_recv.at[x], xa_s.at[d], xa_r.at[d], x_peer(d)))
    x_recv[x] = x_send[x]

    arrive([d_copy])
    real = (iota((512, 256), 0) & 127) < BLK
    draft_l = d_own[...] + d_recv[...]
    d_own[...] = draft_l
    top_d = jnp.max(jnp.where(real, draft_l, -jnp.inf), axis=0, keepdims=True)
    sum_d = jnp.sum(jnp.where(real, jnp.exp(draft_l - top_d), 0.0), axis=0, keepdims=True)

    arrive(x_copies)
    lanes2 = low_lanes((256, 128))
    for j in range(2):
        first, second = x_recv[2 * j].astype(F32), x_recv[2 * j + 1].astype(F32)
        target[:256, j * 128 : j * 128 + 128] = jnp.where(lanes2, first, swap(second))
        target[256:, j * 128 : j * 128 + 128] = jnp.where(lanes2, swap(first), second)

    draft_l, target_l = d_own[...], target[...]
    top_t = jnp.max(jnp.where(real, target_l, -jnp.inf), axis=0, keepdims=True)
    exp_t = jnp.where(real, jnp.exp(target_l - top_t), 0.0)
    sum_t = jnp.sum(exp_t, axis=0, keepdims=True)
    cross = jnp.sum(jnp.where(real, exp_t * (target_l - draft_l), 0.0), axis=0, keepdims=True)

    def packed(stats):
        return jnp.concatenate(list(stats) + [jnp.zeros((8 - len(stats), 256), F32)], axis=0)

    def merge(ref, n):
        part = [ref[i] for i in range(n)]
        top_d, top_t = part[0][0:1], part[0][2:3]
        for p in part[1:]:
            top_d, top_t = jnp.maximum(top_d, p[0:1]), jnp.maximum(top_t, p[2:3])
        sum_d = sum(p[1:2] * jnp.exp(p[0:1] - top_d) for p in part)
        scale = [jnp.exp(p[2:3] - top_t) for p in part]
        sum_t = sum(p[3:4] * s for p, s in zip(part, scale))
        cross = sum(p[4:5] * s for p, s in zip(part, scale))
        return top_d, sum_d, top_t, sum_t, cross

    row_weight_in.wait()
    weights = row_weight_own[...]
    weights = jnp.where(low_lanes((1, 128)) == (c == 0), weights, swap(weights))
    weights = jnp.where(iota((1, 256), 1) >> 6 == x, jnp.concatenate([weights, weights], axis=1), 0.0)
    stat_x[x] = packed((top_d, sum_d, top_t, sum_t, cross, weights))
    copies = [send(stat_x.at[x], stat_x.at[x], sx_s.at[d], sx_r.at[d], x_peer(d)) for d in (2, 1, 3)]
    arrive(copies)
    row_weight = stat_x[0][5:6] + stat_x[1][5:6] + stat_x[2][5:6] + stat_x[3][5:6]
    stat_z[z] = packed(merge(stat_x, 4))
    copies = [
        send(stat_z.at[z], stat_z.at[z], sz_s.at[d], sz_r.at[d], voc_peer(d, 0)) for d in Z_ORDER[:-1]
    ]
    arrive(copies)
    top_d, sum_d, top_t, sum_t, cross = merge(stat_z, 8)
    norm_d = top_d + jnp.log(sum_d)
    norm_t = top_t + jnp.log(sum_t)
    kl = cross / sum_t - norm_t + norm_d
    kl = jnp.where(x < 2, kl[:, :128], kl[:, 128:])
    kl_ref[...] = jnp.where(x % 2 == 0, kl, swap(kl))

    grad_l = row_weight * (jnp.exp(d_own[...] - norm_d) - jnp.exp(target[...] - norm_t))
    grad_l = jnp.where(real, grad_l, 0.0)
    grad[c] = grad_l.astype(BF16)
    g_copy = send(grad.at[c], grad.at[c], gg.at[0], gg.at[1], voc_peer(0, 1))
    grad_t[c] = grad_l.T.astype(BF16).reshape(4, 64, 512)
    arrive([g_copy])
    grad_t[1 - c] = grad[1 - c].astype(F32).T.astype(BF16).reshape(4, 64, 512)

    def ring(buf, mid, fin, me, peer, ss, rr):
        def remote(kind, p, block, dst, d):
            return pltpu.make_async_remote_copy(
                src_ref=buf.at[p, (me + block + 4) % 4], dst_ref=dst, send_sem=ss.at[kind, p],
                recv_sem=rr.at[kind, p], device_id=peer(d), device_id_type=MESH,
            )

        def copies(p, h):
            d = 1 - 2 * h
            return (
                remote(0, p, 2, mid.at[p], d),
                remote(1, p, -d, fin.at[p, 1 - h], -d),
                remote(2, p, d, fin.at[p, h], d),
            )

        def early(p, h):
            far, near, _ = copies(p, h)
            far.start()
            near.start()

        def late(p, h):
            far, _, summed = copies(p, h)
            far.wait_recv()
            block = (me + 1 - 2 * h + 4) % 4
            buf[p, block] = (buf[p, block].astype(F32) + mid[p].astype(F32)).astype(BF16)
            summed.start()

        def total(p, h):
            _, near, summed = copies(p, h)
            near.wait_recv()
            summed.wait_recv()
            return buf[p, me].astype(F32) + fin[p, 0].astype(F32) + fin[p, 1].astype(F32)

        def sent(p, h):
            for copy in copies(p, h):
                copy.wait_send()

        return early, late, total, sent

    x_early, x_late, x_total, x_sent = ring(xs, x_mid, x_fin, x, x_peer, rx_s, rx_r)
    y_early, y_late, y_total, y_sent = ring(ys, y_mid, y_fin, y, y_peer, ry_s, ry_r)

    def columns(p):
        return pl.ds(pl.multiple_of(p * STEP, STEP), STEP)

    def hidden_piece(p):
        right = w_all[:, :, :, columns(p)].reshape(512, STEP)
        out = jnp.dot(grad_t[...].reshape(512, 512), right, preferred_element_type=F32)
        out = out.astype(BF16).reshape(2, 4, 64, STEP)
        for a in range(2):
            for b in range(4):
                xs[p, b, a * 64 : a * 64 + 64, :] = out[a, b]

    def weight_piece(p):
        right = hid_all[:, :, :, columns(p)].reshape(2, 256, STEP)
        out = jnp.dot(grad[0], right[0], preferred_element_type=F32)
        out += jnp.dot(grad[1], right[1], preferred_element_type=F32)
        ys[p] = out.astype(BF16).reshape(4, 128, STEP)

    def z_copy(i, d):
        return pltpu.make_async_remote_copy(
            src_ref=z_send.at[i, (z + d) % 8], dst_ref=z_recv.at[i, z], send_sem=rz_s.at[i, d], recv_sem=rz_r.at[i, d],
            device_id=voc_peer(d, 0), device_id_type=MESH,
        )

    def turn(i, _):
        @pl.when(i < PAIRS)
        def _():
            for h in range(2):
                hidden_piece(2 * i + h)
                x_early(2 * i + h, h)
            for h in range(2):
                weight_piece(2 * i + h)
                y_early(2 * i + h, h)

        @pl.when((i >= 1) & (i < PAIRS + 1))
        def _():
            for h in range(2):
                x_late(2 * i - 2 + h, h)
            for h in range(2):
                y_late(2 * i - 2 + h, h)

        @pl.when(i >= 2)
        def _():
            pair = i - 2
            for h in range(2):
                out = x_total(2 * pair + h, h).astype(BF16)
                z_send[pair, :, :, h * STEP : h * STEP + STEP] = out.reshape(8, 16, STEP)
            for d in Z_ORDER[:-1]:
                z_copy(pair, d).start()
            z_recv[pair, z] = z_send[pair, z]
            for h in range(2):
                gw_ref[:, columns(2 * pair + h)] = y_total(2 * pair + h, h).astype(BF16)

        return 0

    lax.fori_loop(0, PAIRS + 2, turn, 0)

    def finish(i, _):
        for d in Z_ORDER[:-1]:
            z_copy(i, d).wait()
        out = z_recv[i, 0].astype(F32)
        for k in range(1, 8):
            out += z_recv[i, k].astype(F32)
        gh_ref[:, pl.ds(pl.multiple_of(i * 2 * STEP, 2 * STEP), 2 * STEP)] = out.astype(BF16)
        for h in range(2):
            x_sent(2 * i + h, h)
            y_sent(2 * i + h, h)
        return 0

    lax.fori_loop(0, PAIRS, finish, 0)
    drain()


def body(hidden, head_weight, target_logits, vocab_order, draft_map, token_weight):
    tok = lax.axis_index("tok")
    ids = lax.dynamic_slice_in_dim(draft_map, tok * 8 * BLK, 8 * BLK, 0).reshape(8, BLK)
    ids = jnp.pad(ids, ((0, 0), (0, 128 - BLK)), constant_values=-2)
    order = jnp.pad(vocab_order, (0, 63 * 128 - COLS), constant_values=-1).reshape(63, 128)
    in_place = (target_logits.T, hidden.reshape(2, 64, D2), head_weight, token_weight.reshape(1, 128))

    vmem = pl.BlockSpec(memory_space=pltpu.VMEM)
    hbm = pl.BlockSpec(memory_space=pltpu.HBM)
    dma = pltpu.SemaphoreType.DMA
    scratch = [
        pltpu.VMEM((1, 128), F32),
        pltpu.VMEM((BLK, D2), BF16),
        pltpu.VMEM((COLS, 128), BF16),
        pltpu.VMEM((16, 8, 128), I32),
        pltpu.VMEM((128, 128), F32),
        pltpu.VMEM((128, 128), F32),
        pltpu.VMEM((8, 16, 128), BF16),
        pltpu.VMEM((16, 16, 128), BF16),
        pltpu.VMEM((8, 8, 256), I32),
        pltpu.SMEM((8, 8, 256), I32),
        pltpu.VMEM((COLS, 128), F32),
        pltpu.VMEM((8, 256, 128), F32),
        pltpu.VMEM((8, 2, 128, 128), BF16),
        pltpu.VMEM((16, 128, 128), BF16),
        pltpu.VMEM((16, 128), I32),
        pltpu.SMEM((16, 128), I32),
        pltpu.VMEM((4096, 128), F32),
        pltpu.VMEM((16, 128, 128), F32),
        pltpu.VMEM((4, 256, 128), BF16),
        pltpu.VMEM((4, 256, 128), BF16),
        pltpu.VMEM((512, 256), F32),
        pltpu.VMEM((2, 4, 64, D2), BF16),
        pltpu.VMEM((4, 2, 64, D2), BF16),
        pltpu.VMEM((512, 256), F32),
        pltpu.VMEM((512, 256), F32),
        pltpu.VMEM((512, 256), F32),
        pltpu.VMEM((4, 8, 256), F32),
        pltpu.VMEM((8, 8, 256), F32),
        pltpu.VMEM((2, 512, 256), BF16),
        pltpu.VMEM((2, 4, 64, 512), BF16),
        pltpu.VMEM((2 * PAIRS, 4, 128, STEP), BF16),
        pltpu.VMEM((2 * PAIRS, 4, 128, STEP), BF16),
        pltpu.VMEM((2 * PAIRS, 128, STEP), BF16),
        pltpu.VMEM((2 * PAIRS, 128, STEP), BF16),
        pltpu.VMEM((2 * PAIRS, 2, 128, STEP), BF16),
        pltpu.VMEM((2 * PAIRS, 2, 128, STEP), BF16),
        pltpu.VMEM((PAIRS, 8, 16, 2 * STEP), BF16),
        pltpu.VMEM((PAIRS, 8, 16, 2 * STEP), BF16),
        dma((2, 16)),
        dma((12,)), dma((12,)),
        dma((5,)),
        dma((8,)),
        dma((16,)), dma((16,)),
        dma((16,)), dma((16,)),
        dma((4,)), dma((4,)),
        dma((2,)),
        dma((4,)), dma((4,)),
        dma((8,)), dma((8,)),
        dma((2,)),
        dma((3, 2 * PAIRS)), dma((3, 2 * PAIRS)),
        dma((3, 2 * PAIRS)), dma((3, 2 * PAIRS)),
        dma((PAIRS, 8)), dma((PAIRS, 8)),
    ]
    kl, grad_hidden, grad_weight = pl.pallas_call(
        kernel,
        out_shape=(
            jax.ShapeDtypeStruct((1, 128), F32),
            jax.ShapeDtypeStruct((16, D2), BF16),
            jax.ShapeDtypeStruct((128, D2), BF16),
        ),
        in_specs=[vmem, vmem, hbm, hbm, hbm, hbm],
        out_specs=(vmem, vmem, vmem),
        scratch_shapes=scratch,
        compiler_params=pltpu.CompilerParams(
            collective_id=0, has_side_effects=True, vmem_limit_bytes=VMEM_LIMIT
        ),
        name="draft_head",
    )(ids, order, *(pltpu.with_memory_space_constraint(a, pltpu.HBM) for a in in_place))
    return kl[0, :64], grad_hidden, grad_weight[:BLK]


def solution(mesh):
    placed = (
        P("tok", "hid"),
        P(("tok", "voc"), "hid"),
        P("tok", ("voc", "hid")),
        P(("voc", "hid")),
        P(),
        P("tok"),
    )
    return jax.shard_map(
        body,
        mesh=mesh,
        in_specs=placed,
        out_specs=(P(("tok", "hid")), P(("tok", "voc"), "hid"), P(("tok", "voc"), "hid")),
        check_vma=False,
    )
```

```python
import jax
import jax.numpy as jnp
from jax import lax
from jax.experimental import pallas as pl
from jax.experimental.pallas import tpu as pltpu
from jax.sharding import PartitionSpec as P

F32, BF16, I32 = jnp.float32, jnp.bfloat16, jnp.int32
MESH = pl.DeviceIdType.MESH
LOWEST = float(jnp.finfo(jnp.float32).min)
NT = (((1,), (1,)), ((), ()))
COLS = 8016
BLK = 125
D2 = 2048
Z_ORDER = (4, 3, 5, 2, 6, 1, 7, 0)
STEP = 256
PASS_ON = 4
PAIRS = D2 // STEP // 2
VMEM_LIMIT = 48 * 1024 * 1024


def iota(shape, dim):
    return lax.broadcasted_iota(I32, shape, dim)


def low_lanes(shape):
    return iota(shape, 1) < 64


def swap(a):
    return pltpu.roll(a, 64, 1)


def kernel(
    ids_ref, order_ref, logits_ref, hidden_ref, weight_ref, row_weight_ref,
    kl_ref, gh_ref, gw_ref,
    row_weight_own, weight, logits, loc, slot, locz, used, slot_send, slot_recv, src_v, src_s, logits_t, picked, pick_send, pick_recv,
    idx_v, idx_s, rows, placed, x_send, x_recv, target, hid_all, w_all, d_own, d_send, d_recv,
    stat_x, stat_z, t_c, t_z, t_x, c_x, c_z, grad, grad_t, xs, ys, x_mid, y_mid, x_fin, y_fin, z_send, z_recv,
    loc_sem, ag_s, ag_r, copy_sem, src_sem, si_s, si_r, pk_s, pk_r, xa_s, xa_r, dd, sx_s, sx_r, sz_s, sz_r,
    tc, tz_s, tz_r, tx_s, tx_r, cx_s, cx_r, cz_s, cz_r, gg,
    rx_s, rx_r, ry_s, ry_r, rz_s, rz_r,
):
    tok, z, c = lax.axis_index("tok"), lax.axis_index("voc"), lax.axis_index("hid")
    y, x = tok // 4, tok % 4
    shard = z * 2 + c

    def x_peer(d):
        return (y * 4 + (x + d) % 4, z, c)

    def y_peer(d):
        return ((y + d) % 4 * 4 + x, z, c)

    def tok_peer(d):
        return ((tok + d) % 16, z, c)

    def voc_peer(dz, dc):
        return (tok, (z + dz) % 8, (c + dc) % 2)

    unsent, unreceived = [], []

    def send(src, dst, ssem, rsem, peer):
        copy = pltpu.make_async_remote_copy(
            src_ref=src, dst_ref=dst, send_sem=ssem, recv_sem=rsem, device_id=peer, device_id_type=MESH
        )
        copy.start()
        unsent.append(copy)
        unreceived.append(copy)
        return copy

    def arrive(copies):
        for copy in copies:
            copy.wait_recv()
            unreceived[:] = [other for other in unreceived if other is not copy]

    def drain():
        arrive(list(unreceived))
        for copy in unsent:
            copy.wait_send()

    voc_pairs = [(dz, dc) for dz in Z_ORDER for dc in (0, 1) if dz or dc]

    barrier = pltpu.get_barrier_semaphore()
    for d in range(1, 16):
        pl.semaphore_signal(barrier, inc=1, device_id=tok_peer(d), device_id_type=MESH)
    for dz, dc in voc_pairs:
        pl.semaphore_signal(barrier, inc=1, device_id=voc_peer(dz, dc), device_id_type=MESH)

    logits_in = pltpu.make_async_copy(logits_ref, logits, copy_sem.at[0])
    hidden_in = pltpu.make_async_copy(hidden_ref, hid_all.at[:, x], copy_sem.at[1])
    weight_in = pltpu.make_async_copy(weight_ref, weight, copy_sem.at[2])
    row_weight_in = pltpu.make_async_copy(row_weight_ref, row_weight_own, copy_sem.at[3])
    for copy in (weight_in, hidden_in, logits_in, row_weight_in):
        copy.start()

    def join(zz, _):
        wanted = jnp.broadcast_to(ids_ref[pl.ds(zz, 1), :], (128, 128)).T

        def step(b, acc):
            return jnp.where(order_ref[pl.ds(b, 1), :] == wanted, b, acc)

        acc = lax.fori_loop(0, 63, step, jnp.full((128, 128), -1, I32), unroll=9)
        found = jnp.where(acc >= 0, acc * 128 + iota((128, 128), 1), -1).astype(F32)
        loc[tok, pl.ds(zz, 1), :] = jnp.max(found.T, axis=0, keepdims=True).astype(I32)
        return 0

    lax.fori_loop(0, 8, join, 0)

    logits_in.wait()

    def widen(b, _):
        part = pl.ds(pl.multiple_of(b * 48, 48), 48)
        logits_t[part, :] = logits[part, :].astype(F32)
        return 0

    lax.fori_loop(0, COLS // 48, widen, 0, unroll=4)

    pl.semaphore_wait(barrier, 30)
    loc_copies = [
        send(loc.at[tok], loc.at[tok], loc_sem.at[0, d], loc_sem.at[1, d], tok_peer(d)) for d in range(1, 16)
    ]

    weight_in.wait()
    w_all[y, 0] = weight[:64, :]
    w_all[y, 1] = jnp.concatenate([weight[64:, :], jnp.zeros((128 - BLK, D2), BF16)], axis=0)

    def spread(source, first, peer, base):
        copies = []
        for k, (h, d) in enumerate(((0, 1), (1, -1), (1, 1), (0, -1))):
            copies.append(send(source.at[h], first(h, 0), ag_s.at[base + k], ag_r.at[base + k], peer(d)))
        return copies

    def hid_at(h, d):
        return hid_all.at[h, (x + d) % 4]

    def w_at(h, d):
        return w_all.at[(y + d) % 4, h]

    hid_copies = spread(hidden_ref, hid_at, x_peer, 0)
    w_copies = spread(w_all.at[y], w_at, y_peer, 6)

    arrive(loc_copies)

    r0, r1 = iota((128, 128), 0), iota((128, 128), 1)
    before = (r0 < r1).astype(BF16)
    earlier = ((r0 & 7 == (r1 & 7)) & (r1 >> 3 < r0 >> 3)).astype(BF16)
    place = loc[...].reshape(128, 128).astype(F32)
    held = place >= 0.0
    held_b = held.astype(F32).astype(BF16)
    in_row = jnp.dot(held_b, before, preferred_element_type=F32)
    count = jnp.dot(held_b, jnp.ones((128, 128), BF16), preferred_element_type=F32)
    rank = in_row + jnp.dot(earlier, count.astype(BF16), preferred_element_type=F32)
    slot[...] = jnp.where(held, rank, -1.0)
    locz[...] = place
    same = (r0 & 7 == (r1 & 7)).astype(BF16)
    used[...] = jnp.dot(same, count.astype(BF16), preferred_element_type=F32)[:8]
    for zz in range(8):
        slot_send[zz] = slot[pl.ds(zz, 16, stride=8), :].astype(BF16)
    slot_recv[shard] = slot_send[z]

    def list_slots(k):
        zz = (z + Z_ORDER[k]) % 8
        columns = []
        for half in range(2):
            mine = (iota((128, 128), 0) + half * 128).astype(F32)

            def step(t, acc, mine=mine):
                row = pl.ds(t * 8 + zz, 1)
                return jnp.where(slot[row, :] == mine, locz[row, :], acc)

            acc = lax.fori_loop(0, 16, step, jnp.zeros((128, 128), F32), unroll=8)
            columns.append(jnp.sum(acc.T, axis=0, keepdims=True))
        column = jnp.clip(jnp.concatenate(columns, axis=1).astype(I32), 0, COLS - 1)
        src_v[k] = jnp.broadcast_to(column, (8, 256))
        copy = pltpu.make_async_copy(src_v.at[k], src_s.at[k], src_sem.at[k])
        copy.start()
        return copy

    listed = list_slots(0)

    def pass_on(copies, at, peer, base):
        out = []
        for k, d in ((0, -1), (1, 1)):
            arrive([copies[k]])
            out.append(send(at(k, d), at(k, d), ag_s.at[base + 4 + k], ag_r.at[base + 4 + k], peer(-d)))
        return out

    lanes = low_lanes((128, 128))
    pick_copies, slot_copies = [], []
    for k, dz in enumerate(Z_ORDER):
        zz = (z + dz) % 8
        following = list_slots(k + 1) if k < 7 else None
        listed.wait()
        listed = following

        if k == PASS_ON:
            hidden_in.wait()
            hid_more = pass_on(hid_copies, hid_at, x_peer, 0)
            w_more = pass_on(w_copies, w_at, y_peer, 6)
        def pick(g, _, zz=zz, k=k):
            for i in range(16):
                s = g * 16 + i
                picked[zz, pl.ds(s, 1), :] = logits_t[pl.ds(src_s[k, 0, s], 1), :]
            return 0

        lax.fori_loop(0, 16, pick, 0)
        first, second = picked[zz, :128, :], picked[zz, 128:, :]
        pick_send[zz, 0] = jnp.where(lanes, first, swap(second)).astype(BF16)
        pick_send[zz, 1] = jnp.where(lanes, swap(first), second).astype(BF16)
        for dc in (0, 1):
            if dz or dc:
                pick_copies.append(
                    send(
                        pick_send.at[zz, (c + dc) % 2], pick_recv.at[shard],
                        pk_s.at[dz * 2 + dc], pk_r.at[dz * 2 + dc], voc_peer(dz, dc),
                    )
                )
        if k == 1:
            slot_copies = [
                send(
                    slot_send.at[(z + ez) % 8], slot_recv.at[shard],
                    si_s.at[ez * 2 + ec], si_r.at[ez * 2 + ec], voc_peer(ez, ec),
                )
                for ez, ec in voc_pairs
            ]
    pick_recv[shard] = pick_send[z, c]

    def packed(stats):
        width = stats[0].shape[1]
        return jnp.concatenate(list(stats) + [jnp.zeros((8 - len(stats), width), F32)], axis=0)

    def merge(ref, n, row=0):
        part = [ref[i][row : row + 2] for i in range(n)]
        top = part[0][0:1]
        for p in part[1:]:
            top = jnp.maximum(top, p[0:1])
        return top, sum(p[1:2] * jnp.exp(p[0:1] - top) for p in part)

    def to_x(ref, ss, rr):
        return [send(ref.at[x], ref.at[x], ss.at[d], rr.at[d], x_peer(d)) for d in (2, 1, 3)]

    def to_z(ref, ss, rr):
        return [send(ref.at[z], ref.at[z], ss.at[d], rr.at[d], voc_peer(d, 0)) for d in Z_ORDER[:-1]]

    slots_used = used[...]
    seen = picked[...]
    valid = iota((8, 256, 128), 1).astype(F32) < slots_used.reshape(8, 1, 128)
    top_t = jnp.max(jnp.where(valid, seen, LOWEST), axis=(0, 1), keepdims=True)[0]
    sum_t = jnp.sum(jnp.where(valid, jnp.exp(seen - top_t[None]), 0.0), axis=(0, 1), keepdims=True)[0]
    t_c[c] = packed((top_t, sum_t))
    t_copy = send(t_c.at[c], t_c.at[c], tc.at[0], tc.at[1], voc_peer(0, 1))

    arrive(slot_copies)
    index = jnp.zeros((16, 128), F32)
    for s in range(16):
        got = slot_recv[s].astype(F32)
        index = jnp.where(got >= 0.0, got + s * 256.0, index)
    idx_v[...] = jnp.clip(index.astype(I32), 0, 4095)
    to_smem = pltpu.make_async_copy(idx_v, idx_s, copy_sem.at[4])
    to_smem.start()
    to_smem.wait()

    arrive([t_copy])
    t_z[z] = packed(merge(t_c, 2))
    t_copies = to_z(t_z, tz_s, tz_r)

    arrive(hid_copies[2:] + w_copies[2:] + hid_more + w_more)

    def partial_draft(core, out):
        tokens = hid_all[core].reshape(256, D2)

        def step(i, _):
            part = w_all[pl.ds(i * 2, 2)].reshape(256, D2)
            out[pl.ds(pl.multiple_of(i * 256, 256), 256), :] = lax.dot_general(
                part, tokens, NT, preferred_element_type=F32
            )
            return 0

        lax.fori_loop(0, 2, step, 0)

    partial_draft(1 - c, d_send)
    d_copy = send(d_send, d_recv, dd.at[0], dd.at[1], voc_peer(0, 1))
    partial_draft(c, d_own)

    arrive([d_copy])
    real = (iota((512, 256), 0) & 127) < BLK
    draft_l = d_own[...] + d_recv[...]
    d_own[...] = draft_l
    top_d = jnp.max(jnp.where(real, draft_l, -jnp.inf), axis=0, keepdims=True)
    sum_d = jnp.sum(jnp.where(real, jnp.exp(draft_l - top_d), 0.0), axis=0, keepdims=True)
    row_weight_in.wait()
    weights = row_weight_own[...]
    weights = jnp.where(low_lanes((1, 128)) == (c == 0), weights, swap(weights))
    weights = jnp.where(iota((1, 256), 1) >> 6 == x, jnp.concatenate([weights, weights], axis=1), 0.0)
    stat_x[x] = packed((top_d, sum_d, weights))
    d_copies = to_x(stat_x, sx_s, sx_r)

    arrive(pick_copies)

    def unpack(s, _):
        block = pick_recv[s].astype(F32)
        rows[pl.ds(pl.multiple_of(s * 256, 256), 128), :] = block
        rows[pl.ds(pl.multiple_of(s * 256 + 128, 128), 128), :] = swap(block)
        return 0

    lax.fori_loop(0, 16, unpack, 0)

    x_copies = []
    for d in (2, 1, 3, 0):
        xx = (x + d) % 4

        def place_rows(i, _, xx=xx):
            t = (i >> 3) * 4 + xx
            for k in range(16):
                r = (i & 7) * 16 + k
                placed[t, pl.ds(r, 1), :] = rows[pl.ds(idx_s[t, r], 1), :]
            return 0

        lax.fori_loop(0, 32, place_rows, 0)
        for k in range(2):
            x_send[xx, k * 128 : k * 128 + 128, :] = jnp.where(
                lanes, placed[k * 4 + xx], swap(placed[k * 4 + 8 + xx])
            ).astype(BF16)
        if d:
            x_copies.append(send(x_send.at[xx], x_recv.at[x], xa_s.at[d], xa_r.at[d], x_peer(d)))
    x_recv[x] = x_send[x]

    arrive(t_copies)
    top_t, sum_t = merge(t_z, 8)
    t_x[x] = packed((top_t + jnp.log(sum_t),))
    t_copies = to_x(t_x, tx_s, tx_r)
    arrive(d_copies)
    row_weight = stat_x[0][2:3] + stat_x[1][2:3] + stat_x[2][2:3] + stat_x[3][2:3]
    stat_z[z] = packed(merge(stat_x, 4))
    d_copies = to_z(stat_z, sz_s, sz_r)

    arrive(x_copies)
    lanes2 = low_lanes((256, 128))
    for j in range(2):
        first, second = x_recv[2 * j].astype(F32), x_recv[2 * j + 1].astype(F32)
        target[:256, j * 128 : j * 128 + 128] = jnp.where(lanes2, first, swap(second))
        target[256:, j * 128 : j * 128 + 128] = jnp.where(lanes2, swap(first), second)
    arrive(t_copies)
    lanes1 = low_lanes((1, 128))

    def pair_up(first, second):
        return jnp.where(lanes1, jnp.where(c == 0, first, swap(first)), jnp.where(c == 0, swap(second), second))

    norm_t = jnp.concatenate(
        [pair_up(t_x[2 * j][0:1], t_x[2 * j + 1][0:1]) for j in range(2)], axis=1
    )

    arrive(d_copies)
    top_d, sum_d = merge(stat_z, 8)
    norm_d = top_d + jnp.log(sum_d)

    probs = jnp.exp(target[...] - norm_t)
    grad_l = row_weight * (jnp.exp(d_own[...] - norm_d) - probs)
    grad_l = jnp.where(real, grad_l, 0.0)
    grad[c] = grad_l.astype(BF16)
    g_copy = send(grad.at[c], grad.at[c], gg.at[0], gg.at[1], voc_peer(0, 1))
    grad_t[c] = grad_l.T.astype(BF16).reshape(4, 64, 512)
    cross = jnp.sum(jnp.where(real, probs * (target[...] - d_own[...]), 0.0), axis=0, keepdims=True)
    c_x[x] = packed((cross,))
    cross_copies = to_x(c_x, cx_s, cx_r)
    arrive([g_copy])
    grad_t[1 - c] = grad[1 - c].astype(F32).T.astype(BF16).reshape(4, 64, 512)

    def ring(buf, mid, fin, me, peer, ss, rr):
        def remote(kind, p, block, dst, d):
            return pltpu.make_async_remote_copy(
                src_ref=buf.at[p, (me + block + 4) % 4], dst_ref=dst, send_sem=ss.at[kind, p],
                recv_sem=rr.at[kind, p], device_id=peer(d), device_id_type=MESH,
            )

        def copies(p, h):
            d = 1 - 2 * h
            return (
                remote(0, p, 2, mid.at[p], d),
                remote(1, p, -d, fin.at[p, 1 - h], -d),
                remote(2, p, d, fin.at[p, h], d),
            )

        def early(p, h):
            copies(p, h)[0].start()

        def late(p, h):
            far, near, summed = copies(p, h)
            near.start()
            far.wait_recv()
            block = (me + 1 - 2 * h + 4) % 4
            buf[p, block] = (buf[p, block].astype(F32) + mid[p].astype(F32)).astype(BF16)
            summed.start()

        def total(p, h):
            _, near, summed = copies(p, h)
            near.wait_recv()
            summed.wait_recv()
            return buf[p, me].astype(F32) + fin[p, 0].astype(F32) + fin[p, 1].astype(F32)

        def sent(p, h):
            for copy in copies(p, h):
                copy.wait_send()

        return early, late, total, sent

    x_early, x_late, x_total, x_sent = ring(xs, x_mid, x_fin, x, x_peer, rx_s, rx_r)
    y_early, y_late, y_total, y_sent = ring(ys, y_mid, y_fin, y, y_peer, ry_s, ry_r)

    def columns(p):
        return pl.ds(pl.multiple_of(p * STEP, STEP), STEP)

    def hidden_piece(p):
        right = w_all[:, :, :, columns(p)].reshape(512, STEP)
        out = jnp.dot(grad_t[...].reshape(512, 512), right, preferred_element_type=F32)
        out = out.astype(BF16).reshape(2, 4, 64, STEP)
        for a in range(2):
            for b in range(4):
                xs[p, b, a * 64 : a * 64 + 64, :] = out[a, b]

    def weight_piece(p):
        right = hid_all[:, :, :, columns(p)].reshape(2, 256, STEP)
        out = jnp.dot(grad[0], right[0], preferred_element_type=F32)
        out += jnp.dot(grad[1], right[1], preferred_element_type=F32)
        ys[p] = out.astype(BF16).reshape(4, 128, STEP)

    def z_copy(i, d):
        return pltpu.make_async_remote_copy(
            src_ref=z_send.at[i, (z + d) % 8], dst_ref=z_recv.at[i, z], send_sem=rz_s.at[i, d], recv_sem=rz_r.at[i, d],
            device_id=voc_peer(d, 0), device_id_type=MESH,
        )

    def turn(i, _):
        @pl.when(i < PAIRS)
        def _():
            for h in range(2):
                hidden_piece(2 * i + h)
                x_early(2 * i + h, h)
            for h in range(2):
                weight_piece(2 * i + h)
                y_early(2 * i + h, h)

        @pl.when((i >= 1) & (i < PAIRS + 1))
        def _():
            for h in range(2):
                x_late(2 * i - 2 + h, h)
            for h in range(2):
                y_late(2 * i - 2 + h, h)

        @pl.when(i >= 2)
        def _():
            pair = i - 2
            for h in range(2):
                out = x_total(2 * pair + h, h).astype(BF16)
                z_send[pair, :, :, h * STEP : h * STEP + STEP] = out.reshape(8, 16, STEP)
            for d in Z_ORDER[:-1]:
                z_copy(pair, d).start()
            z_recv[pair, z] = z_send[pair, z]
            for h in range(2):
                gw_ref[:, columns(2 * pair + h)] = y_total(2 * pair + h, h).astype(BF16)

        return 0

    lax.fori_loop(0, PAIRS + 2, turn, 0)
    arrive(cross_copies)
    c_z[z] = c_x[0] + c_x[1] + c_x[2] + c_x[3]
    cross_copies = to_z(c_z, cz_s, cz_r)

    def finish(i, _):
        for d in Z_ORDER[:-1]:
            z_copy(i, d).wait()
        out = z_recv[i, 0].astype(F32)
        for k in range(1, 8):
            out += z_recv[i, k].astype(F32)
        gh_ref[:, pl.ds(pl.multiple_of(i * 2 * STEP, 2 * STEP), 2 * STEP)] = out.astype(BF16)
        for h in range(2):
            x_sent(2 * i + h, h)
            y_sent(2 * i + h, h)
        return 0

    lax.fori_loop(0, PAIRS, finish, 0)
    arrive(cross_copies)
    cross = sum(c_z[i][0:1] for i in range(8))
    kl = cross - norm_t + norm_d
    kl = jnp.where(x < 2, kl[:, :128], kl[:, 128:])
    kl_ref[...] = jnp.where(x % 2 == 0, kl, swap(kl))
    drain()


def body(hidden, head_weight, target_logits, vocab_order, draft_map, token_weight):
    tok = lax.axis_index("tok")
    ids = lax.dynamic_slice_in_dim(draft_map, tok * 8 * BLK, 8 * BLK, 0).reshape(8, BLK)
    ids = jnp.pad(ids, ((0, 0), (0, 128 - BLK)), constant_values=-2)
    order = jnp.pad(vocab_order, (0, 63 * 128 - COLS), constant_values=-1).reshape(63, 128)
    in_place = (target_logits.T, hidden.reshape(2, 64, D2), head_weight, token_weight.reshape(1, 128))

    vmem = pl.BlockSpec(memory_space=pltpu.VMEM)
    hbm = pl.BlockSpec(memory_space=pltpu.HBM)
    dma = pltpu.SemaphoreType.DMA
    scratch = [
        pltpu.VMEM((1, 128), F32),
        pltpu.VMEM((BLK, D2), BF16),
        pltpu.VMEM((COLS, 128), BF16),
        pltpu.VMEM((16, 8, 128), I32),
        pltpu.VMEM((128, 128), F32),
        pltpu.VMEM((128, 128), F32),
        pltpu.VMEM((8, 128), F32),
        pltpu.VMEM((8, 16, 128), BF16),
        pltpu.VMEM((16, 16, 128), BF16),
        pltpu.VMEM((8, 8, 256), I32),
        pltpu.SMEM((8, 8, 256), I32),
        pltpu.VMEM((COLS, 128), F32),
        pltpu.VMEM((8, 256, 128), F32),
        pltpu.VMEM((8, 2, 128, 128), BF16),
        pltpu.VMEM((16, 128, 128), BF16),
        pltpu.VMEM((16, 128), I32),
        pltpu.SMEM((16, 128), I32),
        pltpu.VMEM((4096, 128), F32),
        pltpu.VMEM((16, 128, 128), F32),
        pltpu.VMEM((4, 256, 128), BF16),
        pltpu.VMEM((4, 256, 128), BF16),
        pltpu.VMEM((512, 256), F32),
        pltpu.VMEM((2, 4, 64, D2), BF16),
        pltpu.VMEM((4, 2, 64, D2), BF16),
        pltpu.VMEM((512, 256), F32),
        pltpu.VMEM((512, 256), F32),
        pltpu.VMEM((512, 256), F32),
        pltpu.VMEM((4, 8, 256), F32),
        pltpu.VMEM((8, 8, 256), F32),
        pltpu.VMEM((2, 8, 128), F32),
        pltpu.VMEM((8, 8, 128), F32),
        pltpu.VMEM((4, 8, 128), F32),
        pltpu.VMEM((4, 8, 256), F32),
        pltpu.VMEM((8, 8, 256), F32),
        pltpu.VMEM((2, 512, 256), BF16),
        pltpu.VMEM((2, 4, 64, 512), BF16),
        pltpu.VMEM((2 * PAIRS, 4, 128, STEP), BF16),
        pltpu.VMEM((2 * PAIRS, 4, 128, STEP), BF16),
        pltpu.VMEM((2 * PAIRS, 128, STEP), BF16),
        pltpu.VMEM((2 * PAIRS, 128, STEP), BF16),
        pltpu.VMEM((2 * PAIRS, 2, 128, STEP), BF16),
        pltpu.VMEM((2 * PAIRS, 2, 128, STEP), BF16),
        pltpu.VMEM((PAIRS, 8, 16, 2 * STEP), BF16),
        pltpu.VMEM((PAIRS, 8, 16, 2 * STEP), BF16),
        dma((2, 16)),
        dma((12,)), dma((12,)),
        dma((5,)),
        dma((8,)),
        dma((16,)), dma((16,)),
        dma((16,)), dma((16,)),
        dma((4,)), dma((4,)),
        dma((2,)),
        dma((4,)), dma((4,)),
        dma((8,)), dma((8,)),
        dma((2,)),
        dma((8,)), dma((8,)),
        dma((4,)), dma((4,)),
        dma((4,)), dma((4,)),
        dma((8,)), dma((8,)),
        dma((2,)),
        dma((3, 2 * PAIRS)), dma((3, 2 * PAIRS)),
        dma((3, 2 * PAIRS)), dma((3, 2 * PAIRS)),
        dma((PAIRS, 8)), dma((PAIRS, 8)),
    ]
    kl, grad_hidden, grad_weight = pl.pallas_call(
        kernel,
        out_shape=(
            jax.ShapeDtypeStruct((1, 128), F32),
            jax.ShapeDtypeStruct((16, D2), BF16),
            jax.ShapeDtypeStruct((128, D2), BF16),
        ),
        in_specs=[vmem, vmem, hbm, hbm, hbm, hbm],
        out_specs=(vmem, vmem, vmem),
        scratch_shapes=scratch,
        compiler_params=pltpu.CompilerParams(
            collective_id=0, has_side_effects=True, vmem_limit_bytes=VMEM_LIMIT
        ),
        name="draft_head",
    )(ids, order, *(pltpu.with_memory_space_constraint(a, pltpu.HBM) for a in in_place))
    return kl[0, :64], grad_hidden, grad_weight[:BLK]


def solution(mesh):
    placed = (
        P("tok", "hid"),
        P(("tok", "voc"), "hid"),
        P("tok", ("voc", "hid")),
        P(("voc", "hid")),
        P(),
        P("tok"),
    )
    return jax.shard_map(
        body,
        mesh=mesh,
        in_specs=placed,
        out_specs=(P(("tok", "hid")), P(("tok", "voc"), "hid"), P(("tok", "voc"), "hid")),
        check_vma=False,
    )
```

```python
import jax
import jax.numpy as jnp
from jax import lax
from jax.experimental import pallas as pl
from jax.experimental.pallas import tpu as pltpu
from jax.sharding import PartitionSpec as P

F32, BF16, I32 = jnp.float32, jnp.bfloat16, jnp.int32
MESH = pl.DeviceIdType.MESH
LOWEST = float(jnp.finfo(jnp.float32).min)
NT = (((1,), (1,)), ((), ()))
COLS = 8016
BLK = 125
D2 = 2048
Z_ORDER = (4, 3, 5, 2, 6, 1, 7, 0)
STEP = 256
PASS_ON = 4
PAIRS = D2 // STEP // 2
LAST = 2 * PAIRS - 1
VMEM_LIMIT = 48 * 1024 * 1024


def iota(shape, dim):
    return lax.broadcasted_iota(I32, shape, dim)


def low_lanes(shape):
    return iota(shape, 1) < 64


def swap(a):
    return pltpu.roll(a, 64, 1)


def kernel(
    ids_ref, order_ref, logits_ref, hidden_ref, weight_ref, row_weight_ref,
    kl_ref, gh_ref, gw_ref,
    row_weight_own, weight, logits, loc, slot, locz, used, slot_send, slot_recv, src_v, src_s, logits_t, picked, pick_send, pick_recv,
    idx_v, idx_s, rows, placed, x_send, x_recv, target, hid_all, w_all, d_own, d_send, d_recv,
    stat_x, stat_z, t_c, t_z, t_x, c_x, c_z, grad, grad_t, xs, ys, x_mid, y_mid, x_fin, y_fin, z_send, z_recv, zf_send, zf_recv, xf_send, xf_recv,
    loc_sem, ag_s, ag_r, copy_sem, src_sem, si_s, si_r, pk_s, pk_r, xa_s, xa_r, dd, sx_s, sx_r, sz_s, sz_r,
    tc, tz_s, tz_r, tx_s, tx_r, cx_s, cx_r, cz_s, cz_r, gg,
    rx_s, rx_r, ry_s, ry_r, rz_s, rz_r,
    zf_s, zf_r, xf_s, xf_r,
):
    tok, z, c = lax.axis_index("tok"), lax.axis_index("voc"), lax.axis_index("hid")
    y, x = tok // 4, tok % 4
    shard = z * 2 + c

    def x_peer(d):
        return (y * 4 + (x + d) % 4, z, c)

    def y_peer(d):
        return ((y + d) % 4 * 4 + x, z, c)

    def tok_peer(d):
        return ((tok + d) % 16, z, c)

    def voc_peer(dz, dc):
        return (tok, (z + dz) % 8, (c + dc) % 2)

    unsent, unreceived = [], []

    def send(src, dst, ssem, rsem, peer):
        copy = pltpu.make_async_remote_copy(
            src_ref=src, dst_ref=dst, send_sem=ssem, recv_sem=rsem, device_id=peer, device_id_type=MESH
        )
        copy.start()
        unsent.append(copy)
        unreceived.append(copy)
        return copy

    def arrive(copies):
        for copy in copies:
            copy.wait_recv()
            unreceived[:] = [other for other in unreceived if other is not copy]

    def drain():
        arrive(list(unreceived))
        for copy in unsent:
            copy.wait_send()

    voc_pairs = [(dz, dc) for dz in Z_ORDER for dc in (0, 1) if dz or dc]

    barrier = pltpu.get_barrier_semaphore()
    for d in range(1, 16):
        pl.semaphore_signal(barrier, inc=1, device_id=tok_peer(d), device_id_type=MESH)
    for dz, dc in voc_pairs:
        pl.semaphore_signal(barrier, inc=1, device_id=voc_peer(dz, dc), device_id_type=MESH)

    logits_in = pltpu.make_async_copy(logits_ref, logits, copy_sem.at[0])
    hidden_in = pltpu.make_async_copy(hidden_ref, hid_all.at[:, x], copy_sem.at[1])
    weight_in = pltpu.make_async_copy(weight_ref, weight, copy_sem.at[2])
    row_weight_in = pltpu.make_async_copy(row_weight_ref, row_weight_own, copy_sem.at[3])
    for copy in (weight_in, hidden_in, logits_in, row_weight_in):
        copy.start()

    lane = iota((128, 128), 1)
    ids_t = jnp.concatenate([ids_ref[...], jnp.zeros((120, 128), I32)], axis=0).T
    best = jnp.zeros((128, 128), F32)
    for zz in range(8):
        wanted = jnp.broadcast_to(ids_t[:, zz : zz + 1], (128, 128))

        def step(b, acc, wanted=wanted):
            return jnp.where(order_ref[pl.ds(b, 1), :] == wanted, b, acc)

        acc = lax.fori_loop(0, 63, step, jnp.full((128, 128), -1, I32), unroll=9)
        found = jnp.where(acc >= 0, acc * 128 + lane, -1).astype(F32)
        best = jnp.where(lane == zz, jnp.max(found, axis=1, keepdims=True), best)
    loc[tok] = best.T[:8].astype(I32)

    pl.semaphore_wait(barrier, 30)
    loc_copies = [
        send(loc.at[tok], loc.at[tok], loc_sem.at[0, d], loc_sem.at[1, d], tok_peer(d)) for d in range(1, 16)
    ]

    weight_in.wait()
    w_all[y, 0] = weight[:64, :]
    w_all[y, 1] = jnp.concatenate([weight[64:, :], jnp.zeros((128 - BLK, D2), BF16)], axis=0)

    def spread(source, first, peer, base):
        copies = []
        for k, (h, d) in enumerate(((0, 1), (1, -1), (1, 1), (0, -1))):
            copies.append(send(source.at[h], first(h, 0), ag_s.at[base + k], ag_r.at[base + k], peer(d)))
        return copies

    def hid_at(h, d):
        return hid_all.at[h, (x + d) % 4]

    def w_at(h, d):
        return w_all.at[(y + d) % 4, h]

    hid_copies = spread(hidden_ref, hid_at, x_peer, 0)
    w_copies = spread(w_all.at[y], w_at, y_peer, 6)

    logits_in.wait()

    def widen(b, _):
        part = pl.ds(pl.multiple_of(b * 48, 48), 48)
        logits_t[part, :] = logits[part, :].astype(F32)
        return 0

    lax.fori_loop(0, COLS // 48, widen, 0, unroll=4)

    arrive(loc_copies)

    r0, r1 = iota((128, 128), 0), iota((128, 128), 1)
    before = (r0 < r1).astype(BF16)
    earlier = ((r0 & 7 == (r1 & 7)) & (r1 >> 3 < r0 >> 3)).astype(BF16)
    place = loc[...].reshape(128, 128).astype(F32)
    held = place >= 0.0
    held_b = held.astype(F32).astype(BF16)
    in_row = jnp.dot(held_b, before, preferred_element_type=F32)
    count = jnp.dot(held_b, jnp.ones((128, 128), BF16), preferred_element_type=F32)
    rank = in_row + jnp.dot(earlier, count.astype(BF16), preferred_element_type=F32)
    slot[...] = jnp.where(held, rank, -1.0)
    locz[...] = place
    same = (r0 & 7 == (r1 & 7)).astype(BF16)
    used[...] = jnp.dot(same, count.astype(BF16), preferred_element_type=F32)[:8]
    for zz in range(8):
        slot_send[zz] = slot[pl.ds(zz, 16, stride=8), :].astype(BF16)
    slot_recv[shard] = slot_send[z]

    def list_slots(k):
        zz = (z + Z_ORDER[k]) % 8
        columns = []
        for half in range(2):
            mine = (iota((128, 128), 0) + half * 128).astype(F32)

            def step(t, acc, mine=mine):
                row = pl.ds(t * 8 + zz, 1)
                return jnp.where(slot[row, :] == mine, locz[row, :], acc)

            acc = lax.fori_loop(0, 16, step, jnp.zeros((128, 128), F32), unroll=8)
            columns.append(jnp.sum(acc.T, axis=0, keepdims=True))
        column = jnp.clip(jnp.concatenate(columns, axis=1).astype(I32), 0, COLS - 1)
        src_v[k] = jnp.broadcast_to(column, (8, 256))
        copy = pltpu.make_async_copy(src_v.at[k], src_s.at[k], src_sem.at[k])
        copy.start()
        return copy

    listed = list_slots(0)

    def pass_on(copies, at, peer, base):
        out = []
        for k, d in ((0, -1), (1, 1)):
            arrive([copies[k]])
            out.append(send(at(k, d), at(k, d), ag_s.at[base + 4 + k], ag_r.at[base + 4 + k], peer(-d)))
        return out

    lanes = low_lanes((128, 128))
    pick_copies, slot_copies = [], []
    for k, dz in enumerate(Z_ORDER):
        zz = (z + dz) % 8
        following = list_slots(k + 1) if k < 7 else None
        listed.wait()
        listed = following

        if k == PASS_ON:
            hidden_in.wait()
            hid_more = pass_on(hid_copies, hid_at, x_peer, 0)
            w_more = pass_on(w_copies, w_at, y_peer, 6)
        def pick(g, _, zz=zz, k=k):
            for i in range(16):
                s = g * 16 + i
                picked[zz, pl.ds(s, 1), :] = logits_t[pl.ds(src_s[k, 0, s], 1), :]
            return 0

        lax.fori_loop(0, 16, pick, 0)
        first, second = picked[zz, :128, :], picked[zz, 128:, :]
        pick_send[zz, 0] = jnp.where(lanes, first, swap(second)).astype(BF16)
        pick_send[zz, 1] = jnp.where(lanes, swap(first), second).astype(BF16)
        for dc in (0, 1):
            if dz or dc:
                pick_copies.append(
                    send(
                        pick_send.at[zz, (c + dc) % 2], pick_recv.at[shard],
                        pk_s.at[dz * 2 + dc], pk_r.at[dz * 2 + dc], voc_peer(dz, dc),
                    )
                )
        if k == 1:
            slot_copies = [
                send(
                    slot_send.at[(z + ez) % 8], slot_recv.at[shard],
                    si_s.at[ez * 2 + ec], si_r.at[ez * 2 + ec], voc_peer(ez, ec),
                )
                for ez, ec in voc_pairs
            ]
    pick_recv[shard] = pick_send[z, c]

    def packed(stats):
        width = stats[0].shape[1]
        return jnp.concatenate(list(stats) + [jnp.zeros((8 - len(stats), width), F32)], axis=0)

    def merge(ref, n, row=0):
        part = [ref[i][row : row + 2] for i in range(n)]
        top = part[0][0:1]
        for p in part[1:]:
            top = jnp.maximum(top, p[0:1])
        return top, sum(p[1:2] * jnp.exp(p[0:1] - top) for p in part)

    def to_x(ref, ss, rr):
        return [send(ref.at[x], ref.at[x], ss.at[d], rr.at[d], x_peer(d)) for d in (2, 1, 3)]

    def to_z(ref, ss, rr):
        return [send(ref.at[z], ref.at[z], ss.at[d], rr.at[d], voc_peer(d, 0)) for d in Z_ORDER[:-1]]

    slots_used = used[...]
    seen = picked[...]
    valid = iota((8, 256, 128), 1).astype(F32) < slots_used.reshape(8, 1, 128)
    top_t = jnp.max(jnp.where(valid, seen, LOWEST), axis=(0, 1), keepdims=True)[0]
    sum_t = jnp.sum(jnp.where(valid, jnp.exp(seen - top_t[None]), 0.0), axis=(0, 1), keepdims=True)[0]
    t_c[c] = packed((top_t, sum_t))
    t_copy = send(t_c.at[c], t_c.at[c], tc.at[0], tc.at[1], voc_peer(0, 1))

    arrive(slot_copies)
    index = jnp.zeros((16, 128), F32)
    for s in range(16):
        got = slot_recv[s].astype(F32)
        index = jnp.where(got >= 0.0, got + s * 256.0, index)
    idx_v[...] = jnp.clip(index.astype(I32), 0, 4095)
    to_smem = pltpu.make_async_copy(idx_v, idx_s, copy_sem.at[4])
    to_smem.start()
    to_smem.wait()

    arrive([t_copy])
    t_z[z] = packed(merge(t_c, 2))
    t_copies = to_z(t_z, tz_s, tz_r)

    arrive(hid_copies[2:] + w_copies[2:] + hid_more + w_more)

    def partial_draft(core, out):
        tokens = hid_all[core].reshape(256, D2)

        def step(i, _):
            part = w_all[pl.ds(i * 2, 2)].reshape(256, D2)
            out[pl.ds(pl.multiple_of(i * 256, 256), 256), :] = lax.dot_general(
                part, tokens, NT, preferred_element_type=F32
            )
            return 0

        lax.fori_loop(0, 2, step, 0)

    partial_draft(1 - c, d_send)
    d_copy = send(d_send, d_recv, dd.at[0], dd.at[1], voc_peer(0, 1))
    partial_draft(c, d_own)

    arrive([d_copy])
    real = (iota((512, 256), 0) & 127) < BLK
    draft_l = d_own[...] + d_recv[...]
    d_own[...] = draft_l
    top_d = jnp.max(jnp.where(real, draft_l, -jnp.inf), axis=0, keepdims=True)
    sum_d = jnp.sum(jnp.where(real, jnp.exp(draft_l - top_d), 0.0), axis=0, keepdims=True)
    row_weight_in.wait()
    weights = row_weight_own[...]
    weights = jnp.where(low_lanes((1, 128)) == (c == 0), weights, swap(weights))
    weights = jnp.where(iota((1, 256), 1) >> 6 == x, jnp.concatenate([weights, weights], axis=1), 0.0)
    stat_x[x] = packed((top_d, sum_d, weights))
    d_copies = to_x(stat_x, sx_s, sx_r)

    arrive(pick_copies)

    def unpack(s, _):
        block = pick_recv[s].astype(F32)
        rows[pl.ds(pl.multiple_of(s * 256, 256), 128), :] = block
        rows[pl.ds(pl.multiple_of(s * 256 + 128, 128), 128), :] = swap(block)
        return 0

    lax.fori_loop(0, 16, unpack, 0)

    x_copies = []
    for d in (2, 1, 3, 0):
        xx = (x + d) % 4

        def place_rows(i, _, xx=xx):
            t = (i >> 3) * 4 + xx
            for k in range(16):
                r = (i & 7) * 16 + k
                placed[t, pl.ds(r, 1), :] = rows[pl.ds(idx_s[t, r], 1), :]
            return 0

        lax.fori_loop(0, 32, place_rows, 0)
        for k in range(2):
            x_send[xx, k * 128 : k * 128 + 128, :] = jnp.where(
                lanes, placed[k * 4 + xx], swap(placed[k * 4 + 8 + xx])
            ).astype(BF16)
        if d:
            x_copies.append(send(x_send.at[xx], x_recv.at[x], xa_s.at[d], xa_r.at[d], x_peer(d)))
    x_recv[x] = x_send[x]

    arrive(t_copies)
    top_t, sum_t = merge(t_z, 8)
    t_x[x] = packed((top_t + jnp.log(sum_t),))
    t_copies = to_x(t_x, tx_s, tx_r)
    arrive(d_copies)
    row_weight = stat_x[0][2:3] + stat_x[1][2:3] + stat_x[2][2:3] + stat_x[3][2:3]
    stat_z[z] = packed(merge(stat_x, 4))
    d_copies = to_z(stat_z, sz_s, sz_r)

    arrive(x_copies)
    lanes2 = low_lanes((256, 128))
    for j in range(2):
        first, second = x_recv[2 * j].astype(F32), x_recv[2 * j + 1].astype(F32)
        target[:256, j * 128 : j * 128 + 128] = jnp.where(lanes2, first, swap(second))
        target[256:, j * 128 : j * 128 + 128] = jnp.where(lanes2, swap(first), second)
    arrive(t_copies)
    lanes1 = low_lanes((1, 128))

    def pair_up(first, second):
        return jnp.where(lanes1, jnp.where(c == 0, first, swap(first)), jnp.where(c == 0, swap(second), second))

    norm_t = jnp.concatenate(
        [pair_up(t_x[2 * j][0:1], t_x[2 * j + 1][0:1]) for j in range(2)], axis=1
    )

    arrive(d_copies)
    top_d, sum_d = merge(stat_z, 8)
    norm_d = top_d + jnp.log(sum_d)

    probs = jnp.exp(target[...] - norm_t)
    grad_l = row_weight * (jnp.exp(d_own[...] - norm_d) - probs)
    grad_l = jnp.where(real, grad_l, 0.0)
    grad[c] = grad_l.astype(BF16)
    g_copy = send(grad.at[c], grad.at[c], gg.at[0], gg.at[1], voc_peer(0, 1))
    grad_t[c] = grad_l.T.astype(BF16).reshape(4, 64, 512)
    cross = jnp.sum(jnp.where(real, probs * (target[...] - d_own[...]), 0.0), axis=0, keepdims=True)
    c_x[x] = packed((cross,))
    cross_copies = to_x(c_x, cx_s, cx_r)
    arrive([g_copy])
    grad_t[1 - c] = grad[1 - c].astype(F32).T.astype(BF16).reshape(4, 64, 512)

    def ring(buf, mid, fin, me, peer, ss, rr):
        def remote(kind, p, block, dst, d):
            return pltpu.make_async_remote_copy(
                src_ref=buf.at[p, (me + block + 4) % 4], dst_ref=dst, send_sem=ss.at[kind, p],
                recv_sem=rr.at[kind, p], device_id=peer(d), device_id_type=MESH,
            )

        def copies(p, h):
            d = 1 - 2 * h
            return (
                remote(0, p, 2, mid.at[p], d),
                remote(1, p, -d, fin.at[p, 1 - h], -d),
                remote(2, p, d, fin.at[p, h], d),
            )

        def early(p, h):
            copies(p, h)[0].start()

        def late(p, h):
            far, near, summed = copies(p, h)
            near.start()
            far.wait_recv()
            block = (me + 1 - 2 * h + 4) % 4
            buf[p, block] = (buf[p, block].astype(F32) + mid[p].astype(F32)).astype(BF16)
            summed.start()

        def total(p, h):
            _, near, summed = copies(p, h)
            near.wait_recv()
            summed.wait_recv()
            return buf[p, me].astype(F32) + fin[p, 0].astype(F32) + fin[p, 1].astype(F32)

        def sent(p, h):
            for copy in copies(p, h):
                copy.wait_send()

        return early, late, total, sent

    x_early, x_late, x_total, x_sent = ring(xs, x_mid, x_fin, x, x_peer, rx_s, rx_r)
    y_early, y_late, y_total, y_sent = ring(ys, y_mid, y_fin, y, y_peer, ry_s, ry_r)

    def columns(p):
        return pl.ds(pl.multiple_of(p * STEP, STEP), STEP)

    def hidden_product(p):
        right = w_all[:, :, :, columns(p)].reshape(512, STEP)
        out = jnp.dot(grad_t[...].reshape(512, 512), right, preferred_element_type=F32)
        return out.astype(BF16).reshape(2, 4, 64, STEP)

    def hidden_piece(p):
        out = hidden_product(p)
        for a in range(2):
            for b in range(4):
                xs[p, b, a * 64 : a * 64 + 64, :] = out[a, b]

    def weight_piece(p):
        right = hid_all[:, :, :, columns(p)].reshape(2, 256, STEP)
        out = jnp.dot(grad[0], right[0], preferred_element_type=F32)
        out += jnp.dot(grad[1], right[1], preferred_element_type=F32)
        ys[p] = out.astype(BF16).reshape(4, 128, STEP)

    def z_copy(i, d, *part):
        return pltpu.make_async_remote_copy(
            src_ref=z_send.at[(i, (z + d) % 8, *part)], dst_ref=z_recv.at[(i, z, *part)],
            send_sem=rz_s.at[i, d], recv_sem=rz_r.at[i, d], device_id=voc_peer(d, 0), device_id_type=MESH,
        )

    out = hidden_product(LAST)
    for a in range(2):
        for k in range(4):
            for b in range(4):
                zf_send[a * 4 + k, b] = out[a, b, k * 16 : k * 16 + 16]
    zf_copies = [
        send(zf_send.at[(z + d) % 8], zf_recv.at[z], zf_s.at[d], zf_r.at[d], voc_peer(d, 0)) for d in Z_ORDER[:-1]
    ]
    zf_recv[z] = zf_send[z]

    def x_pieces(i, work):
        work(2 * i, 0)
        pl.when(i < PAIRS - 1)(lambda: work(2 * i + 1, 1))

    def turn(i, _):
        @pl.when(i < PAIRS)
        def _():
            def product(p, h):
                hidden_piece(p)
                x_early(p, h)

            x_pieces(i, product)
            for h in range(2):
                weight_piece(2 * i + h)
                y_early(2 * i + h, h)

        @pl.when((i >= 1) & (i < PAIRS + 1))
        def _():
            x_pieces(i - 1, x_late)
            for h in range(2):
                y_late(2 * i - 2 + h, h)

        @pl.when(i >= 2)
        def _():
            pair = i - 2

            def total(p, h):
                z_send[pair, :, h] = x_total(p, h).astype(BF16).reshape(8, 16, STEP)

            x_pieces(pair, total)

            @pl.when(pair < PAIRS - 1)
            def _():
                for d in Z_ORDER[:-1]:
                    z_copy(pair, d).start()
                z_recv[pair, z, 1] = z_send[pair, z, 1]

            @pl.when(pair == PAIRS - 1)
            def _():
                for d in Z_ORDER[:-1]:
                    z_copy(pair, d, 0).start()

            z_recv[pair, z, 0] = z_send[pair, z, 0]
            for h in range(2):
                gw_ref[:, columns(2 * pair + h)] = y_total(2 * pair + h, h).astype(BF16)

        return 0

    lax.fori_loop(0, 3, turn, 0)
    arrive(zf_copies)
    out = zf_recv[0].astype(F32)
    for k in range(1, 8):
        out += zf_recv[k].astype(F32)
    xf_send[...] = out.astype(BF16)
    xf_copies = [
        send(xf_send.at[(x + d) % 4], xf_recv.at[x], xf_s.at[d], xf_r.at[d], x_peer(d)) for d in (2, 1, 3)
    ]
    xf_recv[x] = xf_send[x]
    lax.fori_loop(3, PAIRS + 2, turn, 0)
    arrive(cross_copies)
    c_z[z] = c_x[0] + c_x[1] + c_x[2] + c_x[3]
    cross_copies = to_z(c_z, cz_s, cz_r)

    def summed(i, h):
        out = z_recv[i, 0, h].astype(F32)
        for k in range(1, 8):
            out += z_recv[i, k, h].astype(F32)
        gh_ref[:, columns(2 * i + h)] = out.astype(BF16)

    arrive(xf_copies)
    gh_ref[:, LAST * STEP :] = sum(xf_recv[k].astype(F32) for k in range(4)).astype(BF16)

    def finish(i, _):
        @pl.when(i < PAIRS - 1)
        def _():
            for d in Z_ORDER[:-1]:
                z_copy(i, d).wait()
            summed(i, 1)

        @pl.when(i == PAIRS - 1)
        def _():
            for d in Z_ORDER[:-1]:
                z_copy(i, d, 0).wait()

        summed(i, 0)
        x_pieces(i, x_sent)
        for h in range(2):
            y_sent(2 * i + h, h)
        return 0

    lax.fori_loop(0, PAIRS, finish, 0)
    arrive(cross_copies)
    cross = sum(c_z[i][0:1] for i in range(8))
    kl = cross - norm_t + norm_d
    kl = jnp.where(x < 2, kl[:, :128], kl[:, 128:])
    kl_ref[...] = jnp.where(x % 2 == 0, kl, swap(kl))
    drain()


def body(hidden, head_weight, target_logits, vocab_order, draft_map, token_weight):
    tok = lax.axis_index("tok")
    ids = lax.dynamic_slice_in_dim(draft_map, tok * 8 * BLK, 8 * BLK, 0).reshape(8, BLK)
    ids = jnp.pad(ids, ((0, 0), (0, 128 - BLK)), constant_values=-2)
    order = jnp.pad(vocab_order, (0, 63 * 128 - COLS), constant_values=-1).reshape(63, 128)
    in_place = (target_logits.T, hidden.reshape(2, 64, D2), head_weight, token_weight.reshape(1, 128))

    vmem = pl.BlockSpec(memory_space=pltpu.VMEM)
    hbm = pl.BlockSpec(memory_space=pltpu.HBM)
    dma = pltpu.SemaphoreType.DMA
    scratch = [
        pltpu.VMEM((1, 128), F32),
        pltpu.VMEM((BLK, D2), BF16),
        pltpu.VMEM((COLS, 128), BF16),
        pltpu.VMEM((16, 8, 128), I32),
        pltpu.VMEM((128, 128), F32),
        pltpu.VMEM((128, 128), F32),
        pltpu.VMEM((8, 128), F32),
        pltpu.VMEM((8, 16, 128), BF16),
        pltpu.VMEM((16, 16, 128), BF16),
        pltpu.VMEM((8, 8, 256), I32),
        pltpu.SMEM((8, 8, 256), I32),
        pltpu.VMEM((COLS, 128), F32),
        pltpu.VMEM((8, 256, 128), F32),
        pltpu.VMEM((8, 2, 128, 128), BF16),
        pltpu.VMEM((16, 128, 128), BF16),
        pltpu.VMEM((16, 128), I32),
        pltpu.SMEM((16, 128), I32),
        pltpu.VMEM((4096, 128), F32),
        pltpu.VMEM((16, 128, 128), F32),
        pltpu.VMEM((4, 256, 128), BF16),
        pltpu.VMEM((4, 256, 128), BF16),
        pltpu.VMEM((512, 256), F32),
        pltpu.VMEM((2, 4, 64, D2), BF16),
        pltpu.VMEM((4, 2, 64, D2), BF16),
        pltpu.VMEM((512, 256), F32),
        pltpu.VMEM((512, 256), F32),
        pltpu.VMEM((512, 256), F32),
        pltpu.VMEM((4, 8, 256), F32),
        pltpu.VMEM((8, 8, 256), F32),
        pltpu.VMEM((2, 8, 128), F32),
        pltpu.VMEM((8, 8, 128), F32),
        pltpu.VMEM((4, 8, 128), F32),
        pltpu.VMEM((4, 8, 256), F32),
        pltpu.VMEM((8, 8, 256), F32),
        pltpu.VMEM((2, 512, 256), BF16),
        pltpu.VMEM((2, 4, 64, 512), BF16),
        pltpu.VMEM((2 * PAIRS, 4, 128, STEP), BF16),
        pltpu.VMEM((2 * PAIRS, 4, 128, STEP), BF16),
        pltpu.VMEM((2 * PAIRS, 128, STEP), BF16),
        pltpu.VMEM((2 * PAIRS, 128, STEP), BF16),
        pltpu.VMEM((2 * PAIRS, 2, 128, STEP), BF16),
        pltpu.VMEM((2 * PAIRS, 2, 128, STEP), BF16),
        pltpu.VMEM((PAIRS, 8, 2, 16, STEP), BF16),
        pltpu.VMEM((PAIRS, 8, 2, 16, STEP), BF16),
        pltpu.VMEM((8, 4, 16, STEP), BF16),
        pltpu.VMEM((8, 4, 16, STEP), BF16),
        pltpu.VMEM((4, 16, STEP), BF16),
        pltpu.VMEM((4, 16, STEP), BF16),
        dma((2, 16)),
        dma((12,)), dma((12,)),
        dma((5,)),
        dma((8,)),
        dma((16,)), dma((16,)),
        dma((16,)), dma((16,)),
        dma((4,)), dma((4,)),
        dma((2,)),
        dma((4,)), dma((4,)),
        dma((8,)), dma((8,)),
        dma((2,)),
        dma((8,)), dma((8,)),
        dma((4,)), dma((4,)),
        dma((4,)), dma((4,)),
        dma((8,)), dma((8,)),
        dma((2,)),
        dma((3, 2 * PAIRS)), dma((3, 2 * PAIRS)),
        dma((3, 2 * PAIRS)), dma((3, 2 * PAIRS)),
        dma((PAIRS, 8)), dma((PAIRS, 8)),
        dma((8,)), dma((8,)),
        dma((4,)), dma((4,)),
    ]
    kl, grad_hidden, grad_weight = pl.pallas_call(
        kernel,
        out_shape=(
            jax.ShapeDtypeStruct((1, 128), F32),
            jax.ShapeDtypeStruct((16, D2), BF16),
            jax.ShapeDtypeStruct((128, D2), BF16),
        ),
        in_specs=[vmem, vmem, hbm, hbm, hbm, hbm],
        out_specs=(vmem, vmem, vmem),
        scratch_shapes=scratch,
        compiler_params=pltpu.CompilerParams(
            collective_id=0, has_side_effects=True, vmem_limit_bytes=VMEM_LIMIT
        ),
        name="draft_head",
    )(ids, order, *(pltpu.with_memory_space_constraint(a, pltpu.HBM) for a in in_place))
    return kl[0, :64], grad_hidden, grad_weight[:BLK]


def solution(mesh):
    placed = (
        P("tok", "hid"),
        P(("tok", "voc"), "hid"),
        P("tok", ("voc", "hid")),
        P(("voc", "hid")),
        P(),
        P("tok"),
    )
    return jax.shard_map(
        body,
        mesh=mesh,
        in_specs=placed,
        out_specs=(P(("tok", "hid")), P(("tok", "voc"), "hid"), P(("tok", "voc"), "hid")),
        check_vma=False,
    )
```

```python
import jax
import jax.numpy as jnp
from jax import lax
from jax.experimental import pallas as pl
from jax.experimental.pallas import tpu as pltpu
from jax.sharding import PartitionSpec as P

F32, BF16, I32 = jnp.float32, jnp.bfloat16, jnp.int32
MESH = pl.DeviceIdType.MESH
LOWEST = float(jnp.finfo(jnp.float32).min)
NT = (((1,), (1,)), ((), ()))
COLS = 8016
BLK = 125
D2 = 2048
Z_ORDER = (4, 3, 5, 2, 6, 1, 7, 0)
STEP = 256
PASS_ON = 4
PAIRS = D2 // STEP // 2
LAST = 2 * PAIRS - 1
VMEM_LIMIT = 48 * 1024 * 1024


def iota(shape, dim):
    return lax.broadcasted_iota(I32, shape, dim)


def low_lanes(shape):
    return iota(shape, 1) < 64


def swap(a):
    return pltpu.roll(a, 64, 1)


def kernel(
    ids_ref, order_ref, logits_ref, hidden_ref, weight_ref, row_weight_ref,
    kl_ref, gh_ref, gw_ref,
    row_weight_own, weight, logits, loc, slot, locz, used, slot_send, slot_recv, src_v, src_s, logits_t, picked, pick_send, pick_recv,
    idx_v, idx_s, rows, placed, x_send, x_recv, target, hid_all, w_all, d_own, d_send, d_recv,
    stat_x, stat_z, t_c, t_z, t_x, c_x, c_z, grad, grad_t, xs, ys, x_mid, y_mid, x_fin, y_fin, z_send, z_recv, zf_send, zf_recv, xf_send, xf_recv,
    loc_sem, ag_s, ag_r, copy_sem, src_sem, si_s, si_r, pk_s, pk_r, xa_s, xa_r, dd, sx_s, sx_r, sz_s, sz_r,
    tc, tz_s, tz_r, tx_s, tx_r, cx_s, cx_r, cz_s, cz_r, gg,
    rx_s, rx_r, ry_s, ry_r, rz_s, rz_r,
    zf_s, zf_r, xf_s, xf_r,
):
    tok, z, c = lax.axis_index("tok"), lax.axis_index("voc"), lax.axis_index("hid")
    y, x = tok // 4, tok % 4
    shard = z * 2 + c

    def x_peer(d):
        return (y * 4 + (x + d) % 4, z, c)

    def y_peer(d):
        return ((y + d) % 4 * 4 + x, z, c)

    def tok_peer(d):
        return ((tok + d) % 16, z, c)

    def voc_peer(dz, dc):
        return (tok, (z + dz) % 8, (c + dc) % 2)

    unsent, unreceived = [], []

    def send(src, dst, ssem, rsem, peer):
        copy = pltpu.make_async_remote_copy(
            src_ref=src, dst_ref=dst, send_sem=ssem, recv_sem=rsem, device_id=peer, device_id_type=MESH
        )
        copy.start()
        unsent.append(copy)
        unreceived.append(copy)
        return copy

    def arrive(copies):
        for copy in copies:
            copy.wait_recv()
            unreceived[:] = [other for other in unreceived if other is not copy]

    def drain():
        arrive(list(unreceived))
        for copy in unsent:
            copy.wait_send()

    voc_pairs = [(dz, dc) for dz in Z_ORDER for dc in (0, 1) if dz or dc]

    barrier = pltpu.get_barrier_semaphore()
    for d in range(1, 16):
        pl.semaphore_signal(barrier, inc=1, device_id=tok_peer(d), device_id_type=MESH)
    for dz, dc in voc_pairs:
        pl.semaphore_signal(barrier, inc=1, device_id=voc_peer(dz, dc), device_id_type=MESH)

    logits_in = pltpu.make_async_copy(logits_ref, logits, copy_sem.at[0])
    hidden_in = pltpu.make_async_copy(hidden_ref, hid_all.at[:, x], copy_sem.at[1])
    weight_in = pltpu.make_async_copy(weight_ref, weight, copy_sem.at[2])
    row_weight_in = pltpu.make_async_copy(row_weight_ref, row_weight_own, copy_sem.at[3])
    for copy in (weight_in, hidden_in, logits_in, row_weight_in):
        copy.start()

    lane = iota((128, 128), 1)
    ids_t = jnp.concatenate([ids_ref[...], jnp.zeros((120, 128), I32)], axis=0).T
    best = jnp.zeros((128, 128), F32)
    for zz in range(8):
        wanted = jnp.broadcast_to(ids_t[:, zz : zz + 1], (128, 128))

        def step(b, acc, wanted=wanted):
            return jnp.where(order_ref[pl.ds(b, 1), :] == wanted, b, acc)

        acc = lax.fori_loop(0, 63, step, jnp.full((128, 128), -1, I32), unroll=9)
        found = jnp.where(acc >= 0, acc * 128 + lane, -1).astype(F32)
        best = jnp.where(lane == zz, jnp.max(found, axis=1, keepdims=True), best)
    loc[tok] = best.T[:8].astype(I32)

    pl.semaphore_wait(barrier, 30)
    loc_copies = [
        send(loc.at[tok], loc.at[tok], loc_sem.at[0, d], loc_sem.at[1, d], tok_peer(d)) for d in range(1, 16)
    ]

    weight_in.wait()
    w_all[y, 0] = weight[:64, :]
    w_all[y, 1] = jnp.concatenate([weight[64:, :], jnp.zeros((128 - BLK, D2), BF16)], axis=0)

    def spread(source, first, peer, base):
        copies = []
        for k, (h, d) in enumerate(((0, 1), (1, -1), (1, 1), (0, -1))):
            copies.append(send(source.at[h], first(h, 0), ag_s.at[base + k], ag_r.at[base + k], peer(d)))
        return copies

    def hid_at(h, d):
        return hid_all.at[h, (x + d) % 4]

    def w_at(h, d):
        return w_all.at[(y + d) % 4, h]

    hid_copies = spread(hidden_ref, hid_at, x_peer, 0)
    w_copies = spread(w_all.at[y], w_at, y_peer, 6)

    logits_in.wait()

    def widen(b, _):
        part = pl.ds(pl.multiple_of(b * 48, 48), 48)
        logits_t[part, :] = logits[part, :].astype(F32)
        return 0

    lax.fori_loop(0, COLS // 48, widen, 0, unroll=4)

    arrive(loc_copies)

    r0, r1 = iota((128, 128), 0), iota((128, 128), 1)
    before = (r0 < r1).astype(BF16)
    earlier = ((r0 & 7 == (r1 & 7)) & (r1 >> 3 < r0 >> 3)).astype(BF16)
    place = loc[...].reshape(128, 128).astype(F32)
    held = place >= 0.0
    held_b = held.astype(F32).astype(BF16)
    in_row = jnp.dot(held_b, before, preferred_element_type=F32)
    count = jnp.dot(held_b, jnp.ones((128, 128), BF16), preferred_element_type=F32)
    rank = in_row + jnp.dot(earlier, count.astype(BF16), preferred_element_type=F32)
    slot[...] = jnp.where(held, rank, -1.0)
    locz[...] = place
    same = (r0 & 7 == (r1 & 7)).astype(BF16)
    used[...] = jnp.dot(same, count.astype(BF16), preferred_element_type=F32)[:8]
    for zz in range(8):
        slot_send[zz] = slot[pl.ds(zz, 16, stride=8), :].astype(BF16)
    slot_recv[shard] = slot_send[z]

    def list_slots(k):
        zz = (z + Z_ORDER[k]) % 8
        columns = []
        for half in range(2):
            mine = (iota((128, 128), 0) + half * 128).astype(F32)

            def step(t, acc, mine=mine):
                row = pl.ds(t * 8 + zz, 1)
                return jnp.where(slot[row, :] == mine, locz[row, :], acc)

            acc = lax.fori_loop(0, 16, step, jnp.zeros((128, 128), F32), unroll=8)
            columns.append(jnp.sum(acc.T, axis=0, keepdims=True))
        column = jnp.clip(jnp.concatenate(columns, axis=1).astype(I32), 0, COLS - 1)
        src_v[k] = jnp.broadcast_to(column, (8, 256))
        copy = pltpu.make_async_copy(src_v.at[k], src_s.at[k], src_sem.at[k])
        copy.start()
        return copy

    listed = list_slots(0)

    def pass_on(copies, at, peer, base):
        out = []
        for k, d in ((0, -1), (1, 1)):
            arrive([copies[k]])
            out.append(send(at(k, d), at(k, d), ag_s.at[base + 4 + k], ag_r.at[base + 4 + k], peer(-d)))
        return out

    lanes = low_lanes((128, 128))
    pick_copies, slot_copies = [], []
    for k, dz in enumerate(Z_ORDER):
        zz = (z + dz) % 8
        following = list_slots(k + 1) if k < 7 else None
        listed.wait()
        listed = following

        if k == PASS_ON:
            hidden_in.wait()
            hid_more = pass_on(hid_copies, hid_at, x_peer, 0)
            w_more = pass_on(w_copies, w_at, y_peer, 6)
        def pick(g, _, zz=zz, k=k):
            for i in range(16):
                s = g * 16 + i
                picked[zz, pl.ds(s, 1), :] = logits_t[pl.ds(src_s[k, 0, s], 1), :]
            return 0

        lax.fori_loop(0, 16, pick, 0)
        first, second = picked[zz, :128, :], picked[zz, 128:, :]
        pick_send[zz, 0] = jnp.where(lanes, first, swap(second)).astype(BF16)
        pick_send[zz, 1] = jnp.where(lanes, swap(first), second).astype(BF16)
        for dc in (0, 1):
            if dz or dc:
                pick_copies.append(
                    send(
                        pick_send.at[zz, (c + dc) % 2], pick_recv.at[shard],
                        pk_s.at[dz * 2 + dc], pk_r.at[dz * 2 + dc], voc_peer(dz, dc),
                    )
                )
        if k == 1:
            slot_copies = [
                send(
                    slot_send.at[(z + ez) % 8], slot_recv.at[shard],
                    si_s.at[ez * 2 + ec], si_r.at[ez * 2 + ec], voc_peer(ez, ec),
                )
                for ez, ec in voc_pairs
            ]
    pick_recv[shard] = pick_send[z, c]

    def packed(stats):
        width = stats[0].shape[1]
        return jnp.concatenate(list(stats) + [jnp.zeros((8 - len(stats), width), F32)], axis=0)

    def merge(ref, n, row=0):
        part = [ref[i][row : row + 2] for i in range(n)]
        top = part[0][0:1]
        for p in part[1:]:
            top = jnp.maximum(top, p[0:1])
        return top, sum(p[1:2] * jnp.exp(p[0:1] - top) for p in part)

    def to_x(ref, ss, rr):
        return [send(ref.at[x], ref.at[x], ss.at[d], rr.at[d], x_peer(d)) for d in (2, 1, 3)]

    def to_z(ref, ss, rr):
        return [send(ref.at[z], ref.at[z], ss.at[d], rr.at[d], voc_peer(d, 0)) for d in Z_ORDER[:-1]]

    slots_used = used[...]
    seen = picked[...]
    valid = iota((8, 256, 128), 1).astype(F32) < slots_used.reshape(8, 1, 128)
    top_t = jnp.max(jnp.where(valid, seen, LOWEST), axis=(0, 1), keepdims=True)[0]
    sum_t = jnp.sum(jnp.where(valid, jnp.exp(seen - top_t[None]), 0.0), axis=(0, 1), keepdims=True)[0]
    t_c[c] = packed((top_t, sum_t))
    t_copy = send(t_c.at[c], t_c.at[c], tc.at[0], tc.at[1], voc_peer(0, 1))

    arrive(slot_copies)
    index = jnp.zeros((16, 128), F32)
    for s in range(16):
        got = slot_recv[s].astype(F32)
        index = jnp.where(got >= 0.0, got + s * 256.0, index)
    idx_v[...] = jnp.clip(index.astype(I32), 0, 4095)
    to_smem = pltpu.make_async_copy(idx_v, idx_s, copy_sem.at[4])
    to_smem.start()
    to_smem.wait()

    arrive([t_copy])
    t_z[z] = packed(merge(t_c, 2))
    t_copies = to_z(t_z, tz_s, tz_r)

    arrive(hid_copies[2:] + w_copies[2:] + hid_more + w_more)

    def partial_draft(core, out):
        tokens = hid_all[core].reshape(256, D2)

        def step(i, _):
            part = w_all[pl.ds(i * 2, 2)].reshape(256, D2)
            out[pl.ds(pl.multiple_of(i * 256, 256), 256), :] = lax.dot_general(
                part, tokens, NT, preferred_element_type=F32
            )
            return 0

        lax.fori_loop(0, 2, step, 0)

    partial_draft(1 - c, d_send)
    d_copy = send(d_send, d_recv, dd.at[0], dd.at[1], voc_peer(0, 1))
    partial_draft(c, d_own)

    arrive([d_copy])
    real = (iota((512, 256), 0) & 127) < BLK
    draft_l = d_own[...] + d_recv[...]
    d_own[...] = draft_l
    top_d = jnp.max(jnp.where(real, draft_l, -jnp.inf), axis=0, keepdims=True)
    sum_d = jnp.sum(jnp.where(real, jnp.exp(draft_l - top_d), 0.0), axis=0, keepdims=True)
    row_weight_in.wait()
    weights = row_weight_own[...]
    weights = jnp.where(low_lanes((1, 128)) == (c == 0), weights, swap(weights))
    weights = jnp.where(iota((1, 256), 1) >> 6 == x, jnp.concatenate([weights, weights], axis=1), 0.0)
    stat_x[x] = packed((top_d, sum_d, weights))
    d_copies = to_x(stat_x, sx_s, sx_r)

    arrive(pick_copies)

    def unpack(s, _):
        block = pick_recv[s].astype(F32)
        rows[pl.ds(pl.multiple_of(s * 256, 256), 128), :] = block
        rows[pl.ds(pl.multiple_of(s * 256 + 128, 128), 128), :] = swap(block)
        return 0

    lax.fori_loop(0, 16, unpack, 0)

    x_copies = []
    for d in (2, 1, 3, 0):
        xx = (x + d) % 4

        def place_rows(i, _, xx=xx):
            t = (i >> 3) * 4 + xx
            for k in range(16):
                r = (i & 7) * 16 + k
                placed[t, pl.ds(r, 1), :] = rows[pl.ds(idx_s[t, r], 1), :]
            return 0

        lax.fori_loop(0, 32, place_rows, 0)
        for k in range(2):
            x_send[xx, k * 128 : k * 128 + 128, :] = jnp.where(
                lanes, placed[k * 4 + xx], swap(placed[k * 4 + 8 + xx])
            ).astype(BF16)
        if d:
            x_copies.append(send(x_send.at[xx], x_recv.at[x], xa_s.at[d], xa_r.at[d], x_peer(d)))
    x_recv[x] = x_send[x]

    arrive(t_copies)
    top_t, sum_t = merge(t_z, 8)
    t_x[x] = packed((top_t + jnp.log(sum_t),))
    t_copies = to_x(t_x, tx_s, tx_r)
    arrive(d_copies)
    row_weight = stat_x[0][2:3] + stat_x[1][2:3] + stat_x[2][2:3] + stat_x[3][2:3]
    stat_z[z] = packed(merge(stat_x, 4))
    d_copies = to_z(stat_z, sz_s, sz_r)

    arrive(x_copies)
    lanes2 = low_lanes((256, 128))
    for j in range(2):
        first, second = x_recv[2 * j].astype(F32), x_recv[2 * j + 1].astype(F32)
        target[:256, j * 128 : j * 128 + 128] = jnp.where(lanes2, first, swap(second))
        target[256:, j * 128 : j * 128 + 128] = jnp.where(lanes2, swap(first), second)
    arrive(t_copies)
    lanes1 = low_lanes((1, 128))

    def pair_up(first, second):
        return jnp.where(lanes1, jnp.where(c == 0, first, swap(first)), jnp.where(c == 0, swap(second), second))

    norm_t = jnp.concatenate(
        [pair_up(t_x[2 * j][0:1], t_x[2 * j + 1][0:1]) for j in range(2)], axis=1
    )

    arrive(d_copies)
    top_d, sum_d = merge(stat_z, 8)
    norm_d = top_d + jnp.log(sum_d)

    probs = jnp.exp(target[...] - norm_t)
    grad_l = row_weight * (jnp.exp(d_own[...] - norm_d) - probs)
    grad_l = jnp.where(real, grad_l, 0.0)
    grad[c] = grad_l.astype(BF16)
    g_copy = send(grad.at[c], grad.at[c], gg.at[0], gg.at[1], voc_peer(0, 1))
    grad_t[c] = grad_l.T.astype(BF16).reshape(4, 64, 512)
    cross = jnp.sum(jnp.where(real, probs * (target[...] - d_own[...]), 0.0), axis=0, keepdims=True)
    c_x[x] = packed((cross,))
    cross_copies = to_x(c_x, cx_s, cx_r)
    arrive([g_copy])
    grad_t[1 - c] = grad[1 - c].astype(F32).T.astype(BF16).reshape(4, 64, 512)

    def ring(buf, mid, fin, me, peer, ss, rr):
        def remote(kind, p, block, dst, d):
            return pltpu.make_async_remote_copy(
                src_ref=buf.at[p, (me + block + 4) % 4], dst_ref=dst, send_sem=ss.at[kind, p],
                recv_sem=rr.at[kind, p], device_id=peer(d), device_id_type=MESH,
            )

        def copies(p, h):
            d = 1 - 2 * h
            return (
                remote(0, p, 2, mid.at[p], d),
                remote(1, p, -d, fin.at[p, 1 - h], -d),
                remote(2, p, d, fin.at[p, h], d),
            )

        def early(p, h):
            copies(p, h)[0].start()

        def late(p, h):
            far, near, summed = copies(p, h)
            near.start()
            far.wait_recv()
            block = (me + 1 - 2 * h + 4) % 4
            buf[p, block] = (buf[p, block].astype(F32) + mid[p].astype(F32)).astype(BF16)
            summed.start()

        def total(p, h):
            _, near, summed = copies(p, h)
            near.wait_recv()
            summed.wait_recv()
            return buf[p, me].astype(F32) + fin[p, 0].astype(F32) + fin[p, 1].astype(F32)

        def sent(p, h):
            for copy in copies(p, h):
                copy.wait_send()

        return early, late, total, sent

    x_early, x_late, x_total, x_sent = ring(xs, x_mid, x_fin, x, x_peer, rx_s, rx_r)
    y_early, y_late, y_total, y_sent = ring(ys, y_mid, y_fin, y, y_peer, ry_s, ry_r)

    def columns(p):
        return pl.ds(pl.multiple_of(p * STEP, STEP), STEP)

    def hidden_product(p):
        right = w_all[:, :, :, columns(p)].reshape(512, STEP)
        out = jnp.dot(grad_t[...].reshape(512, 512), right, preferred_element_type=F32)
        return out.astype(BF16).reshape(2, 4, 64, STEP)

    def hidden_piece(p):
        out = hidden_product(p)
        for a in range(2):
            for b in range(4):
                xs[p, b, a * 64 : a * 64 + 64, :] = out[a, b]

    def weight_piece(p):
        right = hid_all[:, :, :, columns(p)].reshape(2, 256, STEP)
        out = jnp.dot(grad[0], right[0], preferred_element_type=F32)
        out += jnp.dot(grad[1], right[1], preferred_element_type=F32)
        ys[p] = out.astype(BF16).reshape(4, 128, STEP)

    def z_copy(i, d, *part):
        return pltpu.make_async_remote_copy(
            src_ref=z_send.at[(i, (z + d) % 8, *part)], dst_ref=z_recv.at[(i, z, *part)],
            send_sem=rz_s.at[i, d], recv_sem=rz_r.at[i, d], device_id=voc_peer(d, 0), device_id_type=MESH,
        )

    def zf_copy(d):
        return pltpu.make_async_remote_copy(
            src_ref=zf_send.at[(z + d) % 8], dst_ref=zf_recv.at[z], send_sem=zf_s.at[d], recv_sem=zf_r.at[d],
            device_id=voc_peer(d, 0), device_id_type=MESH,
        )

    def xf_copy(d):
        return pltpu.make_async_remote_copy(
            src_ref=xf_send.at[(x + d) % 4], dst_ref=xf_recv.at[x], send_sem=xf_s.at[d], recv_sem=xf_r.at[d],
            device_id=x_peer(d), device_id_type=MESH,
        )

    def z_first():
        out = hidden_product(LAST)
        for a in range(2):
            for k in range(4):
                for b in range(4):
                    zf_send[a * 4 + k, b] = out[a, b, k * 16 : k * 16 + 16]
        for d in Z_ORDER[:-1]:
            zf_copy(d).start()
        zf_recv[z] = zf_send[z]

    def x_second():
        for d in Z_ORDER[:-1]:
            zf_copy(d).wait()
        out = zf_recv[0].astype(F32)
        for k in range(1, 8):
            out += zf_recv[k].astype(F32)
        xf_send[...] = out.astype(BF16)
        for d in (2, 1, 3):
            xf_copy(d).start()
        xf_recv[x] = xf_send[x]

    def x_pieces(i, work):
        work(2 * i, 0)
        pl.when(i < PAIRS - 1)(lambda: work(2 * i + 1, 1))

    def turn(i, _):
        @pl.when(i < PAIRS)
        def _():
            def product(p, h):
                hidden_piece(p)
                x_early(p, h)

            x_pieces(i, product)
            for h in range(2):
                weight_piece(2 * i + h)
                y_early(2 * i + h, h)

        pl.when(i == 0)(z_first)
        pl.when(i == 3)(x_second)

        @pl.when((i >= 1) & (i < PAIRS + 1))
        def _():
            x_pieces(i - 1, x_late)
            for h in range(2):
                y_late(2 * i - 2 + h, h)

        @pl.when(i >= 2)
        def _():
            pair = i - 2

            def total(p, h):
                z_send[pair, :, h] = x_total(p, h).astype(BF16).reshape(8, 16, STEP)

            x_pieces(pair, total)

            @pl.when(pair < PAIRS - 1)
            def _():
                for d in Z_ORDER[:-1]:
                    z_copy(pair, d).start()
                z_recv[pair, z, 1] = z_send[pair, z, 1]

            @pl.when(pair == PAIRS - 1)
            def _():
                for d in Z_ORDER[:-1]:
                    z_copy(pair, d, 0).start()

            z_recv[pair, z, 0] = z_send[pair, z, 0]
            for h in range(2):
                gw_ref[:, columns(2 * pair + h)] = y_total(2 * pair + h, h).astype(BF16)

        return 0

    lax.fori_loop(0, PAIRS + 2, turn, 0)
    arrive(cross_copies)
    c_z[z] = c_x[0] + c_x[1] + c_x[2] + c_x[3]
    cross_copies = to_z(c_z, cz_s, cz_r)

    def summed(i, h):
        out = z_recv[i, 0, h].astype(F32)
        for k in range(1, 8):
            out += z_recv[i, k, h].astype(F32)
        gh_ref[:, columns(2 * i + h)] = out.astype(BF16)

    for d in (2, 1, 3):
        xf_copy(d).wait()
    gh_ref[:, LAST * STEP :] = sum(xf_recv[k].astype(F32) for k in range(4)).astype(BF16)

    def finish(i, _):
        @pl.when(i < PAIRS - 1)
        def _():
            for d in Z_ORDER[:-1]:
                z_copy(i, d).wait()
            summed(i, 1)

        @pl.when(i == PAIRS - 1)
        def _():
            for d in Z_ORDER[:-1]:
                z_copy(i, d, 0).wait()

        summed(i, 0)
        x_pieces(i, x_sent)
        for h in range(2):
            y_sent(2 * i + h, h)
        return 0

    lax.fori_loop(0, PAIRS, finish, 0)
    arrive(cross_copies)
    cross = sum(c_z[i][0:1] for i in range(8))
    kl = cross - norm_t + norm_d
    kl = jnp.where(x < 2, kl[:, :128], kl[:, 128:])
    kl_ref[...] = jnp.where(x % 2 == 0, kl, swap(kl))
    drain()


def body(hidden, head_weight, target_logits, vocab_order, draft_map, token_weight):
    tok = lax.axis_index("tok")
    ids = lax.dynamic_slice_in_dim(draft_map, tok * 8 * BLK, 8 * BLK, 0).reshape(8, BLK)
    ids = jnp.pad(ids, ((0, 0), (0, 128 - BLK)), constant_values=-2)
    order = jnp.pad(vocab_order, (0, 63 * 128 - COLS), constant_values=-1).reshape(63, 128)
    in_place = (target_logits.T, hidden.reshape(2, 64, D2), head_weight, token_weight.reshape(1, 128))

    vmem = pl.BlockSpec(memory_space=pltpu.VMEM)
    hbm = pl.BlockSpec(memory_space=pltpu.HBM)
    dma = pltpu.SemaphoreType.DMA
    scratch = [
        pltpu.VMEM((1, 128), F32),
        pltpu.VMEM((BLK, D2), BF16),
        pltpu.VMEM((COLS, 128), BF16),
        pltpu.VMEM((16, 8, 128), I32),
        pltpu.VMEM((128, 128), F32),
        pltpu.VMEM((128, 128), F32),
        pltpu.VMEM((8, 128), F32),
        pltpu.VMEM((8, 16, 128), BF16),
        pltpu.VMEM((16, 16, 128), BF16),
        pltpu.VMEM((8, 8, 256), I32),
        pltpu.SMEM((8, 8, 256), I32),
        pltpu.VMEM((COLS, 128), F32),
        pltpu.VMEM((8, 256, 128), F32),
        pltpu.VMEM((8, 2, 128, 128), BF16),
        pltpu.VMEM((16, 128, 128), BF16),
        pltpu.VMEM((16, 128), I32),
        pltpu.SMEM((16, 128), I32),
        pltpu.VMEM((4096, 128), F32),
        pltpu.VMEM((16, 128, 128), F32),
        pltpu.VMEM((4, 256, 128), BF16),
        pltpu.VMEM((4, 256, 128), BF16),
        pltpu.VMEM((512, 256), F32),
        pltpu.VMEM((2, 4, 64, D2), BF16),
        pltpu.VMEM((4, 2, 64, D2), BF16),
        pltpu.VMEM((512, 256), F32),
        pltpu.VMEM((512, 256), F32),
        pltpu.VMEM((512, 256), F32),
        pltpu.VMEM((4, 8, 256), F32),
        pltpu.VMEM((8, 8, 256), F32),
        pltpu.VMEM((2, 8, 128), F32),
        pltpu.VMEM((8, 8, 128), F32),
        pltpu.VMEM((4, 8, 128), F32),
        pltpu.VMEM((4, 8, 256), F32),
        pltpu.VMEM((8, 8, 256), F32),
        pltpu.VMEM((2, 512, 256), BF16),
        pltpu.VMEM((2, 4, 64, 512), BF16),
        pltpu.VMEM((2 * PAIRS, 4, 128, STEP), BF16),
        pltpu.VMEM((2 * PAIRS, 4, 128, STEP), BF16),
        pltpu.VMEM((2 * PAIRS, 128, STEP), BF16),
        pltpu.VMEM((2 * PAIRS, 128, STEP), BF16),
        pltpu.VMEM((2 * PAIRS, 2, 128, STEP), BF16),
        pltpu.VMEM((2 * PAIRS, 2, 128, STEP), BF16),
        pltpu.VMEM((PAIRS, 8, 2, 16, STEP), BF16),
        pltpu.VMEM((PAIRS, 8, 2, 16, STEP), BF16),
        pltpu.VMEM((8, 4, 16, STEP), BF16),
        pltpu.VMEM((8, 4, 16, STEP), BF16),
        pltpu.VMEM((4, 16, STEP), BF16),
        pltpu.VMEM((4, 16, STEP), BF16),
        dma((2, 16)),
        dma((12,)), dma((12,)),
        dma((5,)),
        dma((8,)),
        dma((16,)), dma((16,)),
        dma((16,)), dma((16,)),
        dma((4,)), dma((4,)),
        dma((2,)),
        dma((4,)), dma((4,)),
        dma((8,)), dma((8,)),
        dma((2,)),
        dma((8,)), dma((8,)),
        dma((4,)), dma((4,)),
        dma((4,)), dma((4,)),
        dma((8,)), dma((8,)),
        dma((2,)),
        dma((3, 2 * PAIRS)), dma((3, 2 * PAIRS)),
        dma((3, 2 * PAIRS)), dma((3, 2 * PAIRS)),
        dma((PAIRS, 8)), dma((PAIRS, 8)),
        dma((8,)), dma((8,)),
        dma((4,)), dma((4,)),
    ]
    kl, grad_hidden, grad_weight = pl.pallas_call(
        kernel,
        out_shape=(
            jax.ShapeDtypeStruct((1, 128), F32),
            jax.ShapeDtypeStruct((16, D2), BF16),
            jax.ShapeDtypeStruct((128, D2), BF16),
        ),
        in_specs=[vmem, vmem, hbm, hbm, hbm, hbm],
        out_specs=(vmem, vmem, vmem),
        scratch_shapes=scratch,
        compiler_params=pltpu.CompilerParams(
            collective_id=0, has_side_effects=True, vmem_limit_bytes=VMEM_LIMIT
        ),
        name="draft_head",
    )(ids, order, *(pltpu.with_memory_space_constraint(a, pltpu.HBM) for a in in_place))
    return kl[0, :64], grad_hidden, grad_weight[:BLK]


def solution(mesh):
    placed = (
        P("tok", "hid"),
        P(("tok", "voc"), "hid"),
        P("tok", ("voc", "hid")),
        P(("voc", "hid")),
        P(),
        P("tok"),
    )
    return jax.shard_map(
        body,
        mesh=mesh,
        in_specs=placed,
        out_specs=(P(("tok", "hid")), P(("tok", "voc"), "hid"), P(("tok", "voc"), "hid")),
        check_vma=False,
    )
```

```python
import jax
import jax.numpy as jnp
from jax import lax
from jax.experimental import pallas as pl
from jax.experimental.pallas import tpu as pltpu
from jax.sharding import PartitionSpec as P

F32, BF16, I32 = jnp.float32, jnp.bfloat16, jnp.int32
MESH = pl.DeviceIdType.MESH
LOWEST = float(jnp.finfo(jnp.float32).min)
NT = (((1,), (1,)), ((), ()))
COLS = 8016
BLK = 125
D2 = 2048
Z_ORDER = (4, 3, 5, 2, 6, 1, 7, 0)
STEP = 256
FAR_FIRST = (10, 6, 9, 11, 14, 5, 7, 2, 8, 13, 15, 1, 3, 4, 12)
PASS_ON = 4
PAIRS = D2 // STEP // 2
LAST = 2 * PAIRS - 1
VMEM_LIMIT = 48 * 1024 * 1024


def iota(shape, dim):
    return lax.broadcasted_iota(I32, shape, dim)


def low_lanes(shape):
    return iota(shape, 1) < 64


def swap(a):
    return pltpu.roll(a, 64, 1)


def kernel(
    ids_ref, order_ref, logits_ref, hidden_ref, weight_ref, row_weight_ref,
    kl_ref, gh_ref, gw_ref,
    row_weight_own, weight, logits, loc, slot, locz, used, slot_send, slot_recv, src_v, src_s, logits_t, picked, pick_send, pick_recv,
    idx_v, idx_s, rows, placed, x_send, x_recv, target, hid_all, w_all, d_own, d_send, d_recv,
    stat_x, stat_z, t_c, t_z, t_x, c_x, c_z, grad, grad_t, xs, ys, x_mid, y_mid, x_fin, y_fin, z_send, z_recv, zf_send, zf_recv, xf_send, xf_recv,
    loc_sem, ag_s, ag_r, copy_sem, src_sem, si_s, si_r, pk_s, pk_r, xa_s, xa_r, dd, sx_s, sx_r, sz_s, sz_r,
    tc, tz_s, tz_r, tx_s, tx_r, cx_s, cx_r, cz_s, cz_r, gg,
    rx_s, rx_r, ry_s, ry_r, rz_s, rz_r,
    zf_s, zf_r, xf_s, xf_r,
):
    tok, z, c = lax.axis_index("tok"), lax.axis_index("voc"), lax.axis_index("hid")
    y, x = tok // 4, tok % 4
    shard = z * 2 + c

    def x_peer(d):
        return (y * 4 + (x + d) % 4, z, c)

    def y_peer(d):
        return ((y + d) % 4 * 4 + x, z, c)

    def tok_peer(d):
        return ((tok + d) % 16, z, c)

    def voc_peer(dz, dc):
        return (tok, (z + dz) % 8, (c + dc) % 2)

    unsent, unreceived = [], []

    def send(src, dst, ssem, rsem, peer):
        copy = pltpu.make_async_remote_copy(
            src_ref=src, dst_ref=dst, send_sem=ssem, recv_sem=rsem, device_id=peer, device_id_type=MESH
        )
        copy.start()
        unsent.append(copy)
        unreceived.append(copy)
        return copy

    def arrive(copies):
        for copy in copies:
            copy.wait_recv()
            unreceived[:] = [other for other in unreceived if other is not copy]

    def drain():
        arrive(list(unreceived))
        for copy in unsent:
            copy.wait_send()

    voc_pairs = [(dz, dc) for dz in Z_ORDER for dc in (0, 1) if dz or dc]

    barrier = pltpu.get_barrier_semaphore()
    for d in range(1, 16):
        pl.semaphore_signal(barrier, inc=1, device_id=tok_peer(d), device_id_type=MESH)
    for dz, dc in voc_pairs:
        pl.semaphore_signal(barrier, inc=1, device_id=voc_peer(dz, dc), device_id_type=MESH)

    logits_in = pltpu.make_async_copy(logits_ref, logits, copy_sem.at[0])
    hidden_in = pltpu.make_async_copy(hidden_ref, hid_all.at[:, x], copy_sem.at[1])
    weight_in = pltpu.make_async_copy(weight_ref, weight, copy_sem.at[2])
    row_weight_in = pltpu.make_async_copy(row_weight_ref, row_weight_own, copy_sem.at[3])
    for copy in (weight_in, hidden_in, logits_in, row_weight_in):
        copy.start()

    lane = iota((128, 128), 1)
    ids_t = jnp.concatenate([ids_ref[...], jnp.zeros((120, 128), I32)], axis=0).T
    best = jnp.zeros((128, 128), F32)
    for zz in range(8):
        wanted = jnp.broadcast_to(ids_t[:, zz : zz + 1], (128, 128))

        def step(b, acc, wanted=wanted):
            return jnp.where(order_ref[pl.ds(b, 1), :] == wanted, b, acc)

        acc = lax.fori_loop(0, 63, step, jnp.full((128, 128), -1, I32), unroll=9)
        found = jnp.where(acc >= 0, acc * 128 + lane, -1).astype(F32)
        best = jnp.where(lane == zz, jnp.max(found, axis=1, keepdims=True), best)
    loc[tok] = best.T[:8].astype(I32)

    pl.semaphore_wait(barrier, 30)
    loc_copies = [
        send(loc.at[tok], loc.at[tok], loc_sem.at[0, d], loc_sem.at[1, d], tok_peer(d)) for d in FAR_FIRST
    ]

    weight_in.wait()
    w_all[y, 0] = weight[:64, :]
    w_all[y, 1] = jnp.concatenate([weight[64:, :], jnp.zeros((128 - BLK, D2), BF16)], axis=0)

    def spread(source, first, peer, base):
        copies = []
        for k, (h, d) in enumerate(((0, 1), (1, -1), (1, 1), (0, -1))):
            copies.append(send(source.at[h], first(h, 0), ag_s.at[base + k], ag_r.at[base + k], peer(d)))
        return copies

    def hid_at(h, d):
        return hid_all.at[h, (x + d) % 4]

    def w_at(h, d):
        return w_all.at[(y + d) % 4, h]

    hid_copies = spread(hidden_ref, hid_at, x_peer, 0)
    w_copies = spread(w_all.at[y], w_at, y_peer, 6)

    logits_in.wait()

    def widen(b, _):
        part = pl.ds(pl.multiple_of(b * 48, 48), 48)
        logits_t[part, :] = logits[part, :].astype(F32)
        return 0

    lax.fori_loop(0, COLS // 48, widen, 0, unroll=4)

    arrive(loc_copies)

    r0, r1 = iota((128, 128), 0), iota((128, 128), 1)
    before = (r0 < r1).astype(BF16)
    earlier = ((r0 & 7 == (r1 & 7)) & (r1 >> 3 < r0 >> 3)).astype(BF16)
    place = loc[...].reshape(128, 128).astype(F32)
    held = place >= 0.0
    held_b = held.astype(F32).astype(BF16)
    in_row = jnp.dot(held_b, before, preferred_element_type=F32)
    count = jnp.dot(held_b, jnp.ones((128, 128), BF16), preferred_element_type=F32)
    rank = in_row + jnp.dot(earlier, count.astype(BF16), preferred_element_type=F32)
    slot[...] = jnp.where(held, rank, -1.0)
    locz[...] = place
    same = (r0 & 7 == (r1 & 7)).astype(BF16)
    used[...] = jnp.dot(same, count.astype(BF16), preferred_element_type=F32)[:8]
    for zz in range(8):
        slot_send[zz] = slot[pl.ds(zz, 16, stride=8), :].astype(BF16)
    slot_recv[shard] = slot_send[z]

    def list_slots(k):
        zz = (z + Z_ORDER[k]) % 8
        columns = []
        for half in range(2):
            mine = (iota((128, 128), 0) + half * 128).astype(F32)

            def step(t, acc, mine=mine):
                row = pl.ds(t * 8 + zz, 1)
                return jnp.where(slot[row, :] == mine, locz[row, :], acc)

            acc = lax.fori_loop(0, 16, step, jnp.zeros((128, 128), F32), unroll=8)
            columns.append(jnp.sum(acc.T, axis=0, keepdims=True))
        column = jnp.clip(jnp.concatenate(columns, axis=1).astype(I32), 0, COLS - 1)
        src_v[k] = jnp.broadcast_to(column, (8, 256))
        copy = pltpu.make_async_copy(src_v.at[k], src_s.at[k], src_sem.at[k])
        copy.start()
        return copy

    listed = list_slots(0)

    def pass_on(copies, at, peer, base):
        out = []
        for k, d in ((0, -1), (1, 1)):
            arrive([copies[k]])
            out.append(send(at(k, d), at(k, d), ag_s.at[base + 4 + k], ag_r.at[base + 4 + k], peer(-d)))
        return out

    lanes = low_lanes((128, 128))
    pick_copies, slot_copies = [], []
    for k, dz in enumerate(Z_ORDER):
        zz = (z + dz) % 8
        following = list_slots(k + 1) if k < 7 else None
        listed.wait()
        listed = following

        if k == PASS_ON:
            hidden_in.wait()
            hid_more = pass_on(hid_copies, hid_at, x_peer, 0)
            w_more = pass_on(w_copies, w_at, y_peer, 6)
        def pick(g, _, zz=zz, k=k):
            for i in range(16):
                s = g * 16 + i
                picked[zz, pl.ds(s, 1), :] = logits_t[pl.ds(src_s[k, 0, s], 1), :]
            return 0

        lax.fori_loop(0, 16, pick, 0)
        first, second = picked[zz, :128, :], picked[zz, 128:, :]
        pick_send[zz, 0] = jnp.where(lanes, first, swap(second)).astype(BF16)
        pick_send[zz, 1] = jnp.where(lanes, swap(first), second).astype(BF16)
        for dc in (0, 1):
            if dz or dc:
                pick_copies.append(
                    send(
                        pick_send.at[zz, (c + dc) % 2], pick_recv.at[shard],
                        pk_s.at[dz * 2 + dc], pk_r.at[dz * 2 + dc], voc_peer(dz, dc),
                    )
                )
        if k == 1:
            slot_copies = [
                send(
                    slot_send.at[(z + ez) % 8], slot_recv.at[shard],
                    si_s.at[ez * 2 + ec], si_r.at[ez * 2 + ec], voc_peer(ez, ec),
                )
                for ez, ec in voc_pairs
            ]
    pick_recv[shard] = pick_send[z, c]

    def packed(stats):
        width = stats[0].shape[1]
        return jnp.concatenate(list(stats) + [jnp.zeros((8 - len(stats), width), F32)], axis=0)

    def merge(ref, n, row=0):
        part = [ref[i][row : row + 2] for i in range(n)]
        top = part[0][0:1]
        for p in part[1:]:
            top = jnp.maximum(top, p[0:1])
        return top, sum(p[1:2] * jnp.exp(p[0:1] - top) for p in part)

    def to_x(ref, ss, rr):
        return [send(ref.at[x], ref.at[x], ss.at[d], rr.at[d], x_peer(d)) for d in (2, 1, 3)]

    def to_z(ref, ss, rr):
        return [send(ref.at[z], ref.at[z], ss.at[d], rr.at[d], voc_peer(d, 0)) for d in Z_ORDER[:-1]]

    slots_used = used[...]
    seen = picked[...]
    valid = iota((8, 256, 128), 1).astype(F32) < slots_used.reshape(8, 1, 128)
    top_t = jnp.max(jnp.where(valid, seen, LOWEST), axis=(0, 1), keepdims=True)[0]
    sum_t = jnp.sum(jnp.where(valid, jnp.exp(seen - top_t[None]), 0.0), axis=(0, 1), keepdims=True)[0]
    t_c[c] = packed((top_t, sum_t))
    t_copy = send(t_c.at[c], t_c.at[c], tc.at[0], tc.at[1], voc_peer(0, 1))

    arrive(slot_copies)
    index = jnp.zeros((16, 128), F32)
    for s in range(16):
        got = slot_recv[s].astype(F32)
        index = jnp.where(got >= 0.0, got + s * 256.0, index)
    idx_v[...] = jnp.clip(index.astype(I32), 0, 4095)
    to_smem = pltpu.make_async_copy(idx_v, idx_s, copy_sem.at[4])
    to_smem.start()
    to_smem.wait()

    arrive([t_copy])
    t_z[z] = packed(merge(t_c, 2))
    t_copies = to_z(t_z, tz_s, tz_r)

    arrive(hid_copies[2:] + w_copies[2:] + hid_more + w_more)

    def partial_draft(core, out):
        tokens = hid_all[core].reshape(256, D2)

        def step(i, _):
            part = w_all[pl.ds(i * 2, 2)].reshape(256, D2)
            out[pl.ds(pl.multiple_of(i * 256, 256), 256), :] = lax.dot_general(
                part, tokens, NT, preferred_element_type=F32
            )
            return 0

        lax.fori_loop(0, 2, step, 0)

    partial_draft(1 - c, d_send)
    d_copy = send(d_send, d_recv, dd.at[0], dd.at[1], voc_peer(0, 1))
    partial_draft(c, d_own)

    arrive([d_copy])
    real = (iota((512, 256), 0) & 127) < BLK
    draft_l = d_own[...] + d_recv[...]
    d_own[...] = draft_l
    top_d = jnp.max(jnp.where(real, draft_l, -jnp.inf), axis=0, keepdims=True)
    sum_d = jnp.sum(jnp.where(real, jnp.exp(draft_l - top_d), 0.0), axis=0, keepdims=True)
    row_weight_in.wait()
    weights = row_weight_own[...]
    weights = jnp.where(low_lanes((1, 128)) == (c == 0), weights, swap(weights))
    weights = jnp.where(iota((1, 256), 1) >> 6 == x, jnp.concatenate([weights, weights], axis=1), 0.0)
    stat_x[x] = packed((top_d, sum_d, weights))
    d_copies = to_x(stat_x, sx_s, sx_r)

    def unpack(s):
        block = pick_recv[s].astype(F32)
        rows[pl.ds(pl.multiple_of(s * 256, 256), 128), :] = block
        rows[pl.ds(pl.multiple_of(s * 256 + 128, 128), 128), :] = swap(block)

    unpack(shard)
    for (dz, dc), copy in zip(voc_pairs, pick_copies):
        arrive([copy])
        unpack((z - dz + 8) % 8 * 2 + (c - dc + 2) % 2)

    x_copies = []
    for d in (2, 1, 3, 0):
        xx = (x + d) % 4

        def place_rows(i, _, xx=xx):
            t = (i >> 3) * 4 + xx
            for k in range(16):
                r = (i & 7) * 16 + k
                placed[t, pl.ds(r, 1), :] = rows[pl.ds(idx_s[t, r], 1), :]
            return 0

        lax.fori_loop(0, 32, place_rows, 0)
        for k in range(2):
            x_send[xx, k * 128 : k * 128 + 128, :] = jnp.where(
                lanes, placed[k * 4 + xx], swap(placed[k * 4 + 8 + xx])
            ).astype(BF16)
        if d:
            x_copies.append(send(x_send.at[xx], x_recv.at[x], xa_s.at[d], xa_r.at[d], x_peer(d)))
    x_recv[x] = x_send[x]

    arrive(t_copies)
    top_t, sum_t = merge(t_z, 8)
    t_x[x] = packed((top_t + jnp.log(sum_t),))
    t_copies = to_x(t_x, tx_s, tx_r)
    arrive(d_copies)
    row_weight = stat_x[0][2:3] + stat_x[1][2:3] + stat_x[2][2:3] + stat_x[3][2:3]
    stat_z[z] = packed(merge(stat_x, 4))
    d_copies = to_z(stat_z, sz_s, sz_r)

    arrive(x_copies)
    lanes2 = low_lanes((256, 128))
    for j in range(2):
        first, second = x_recv[2 * j].astype(F32), x_recv[2 * j + 1].astype(F32)
        target[:256, j * 128 : j * 128 + 128] = jnp.where(lanes2, first, swap(second))
        target[256:, j * 128 : j * 128 + 128] = jnp.where(lanes2, swap(first), second)
    arrive(t_copies)
    lanes1 = low_lanes((1, 128))

    def pair_up(first, second):
        return jnp.where(lanes1, jnp.where(c == 0, first, swap(first)), jnp.where(c == 0, swap(second), second))

    norm_t = jnp.concatenate(
        [pair_up(t_x[2 * j][0:1], t_x[2 * j + 1][0:1]) for j in range(2)], axis=1
    )

    arrive(d_copies)
    top_d, sum_d = merge(stat_z, 8)
    norm_d = top_d + jnp.log(sum_d)

    probs = jnp.exp(target[...] - norm_t)
    grad_l = row_weight * (jnp.exp(d_own[...] - norm_d) - probs)
    grad_l = jnp.where(real, grad_l, 0.0)
    grad[c] = grad_l.astype(BF16)
    g_copy = send(grad.at[c], grad.at[c], gg.at[0], gg.at[1], voc_peer(0, 1))
    grad_t[c] = grad_l.T.astype(BF16).reshape(4, 64, 512)
    cross = jnp.sum(jnp.where(real, probs * (target[...] - d_own[...]), 0.0), axis=0, keepdims=True)
    c_x[x] = packed((cross,))
    cross_copies = to_x(c_x, cx_s, cx_r)
    arrive([g_copy])
    grad_t[1 - c] = grad[1 - c].astype(F32).T.astype(BF16).reshape(4, 64, 512)

    def ring(buf, mid, fin, me, peer, ss, rr):
        def remote(kind, p, block, dst, d):
            return pltpu.make_async_remote_copy(
                src_ref=buf.at[p, (me + block + 4) % 4], dst_ref=dst, send_sem=ss.at[kind, p],
                recv_sem=rr.at[kind, p], device_id=peer(d), device_id_type=MESH,
            )

        def copies(p, h):
            d = 1 - 2 * h
            return (
                remote(0, p, 2, mid.at[p], d),
                remote(1, p, -d, fin.at[p, 1 - h], -d),
                remote(2, p, d, fin.at[p, h], d),
            )

        def early(p, h):
            copies(p, h)[0].start()

        def late(p, h):
            far, near, summed = copies(p, h)
            near.start()
            far.wait_recv()
            block = (me + 1 - 2 * h + 4) % 4
            buf[p, block] = (buf[p, block].astype(F32) + mid[p].astype(F32)).astype(BF16)
            summed.start()

        def total(p, h):
            _, near, summed = copies(p, h)
            near.wait_recv()
            summed.wait_recv()
            return buf[p, me].astype(F32) + fin[p, 0].astype(F32) + fin[p, 1].astype(F32)

        def sent(p, h):
            for copy in copies(p, h):
                copy.wait_send()

        return early, late, total, sent

    x_early, x_late, x_total, x_sent = ring(xs, x_mid, x_fin, x, x_peer, rx_s, rx_r)
    y_early, y_late, y_total, y_sent = ring(ys, y_mid, y_fin, y, y_peer, ry_s, ry_r)

    def columns(p):
        return pl.ds(pl.multiple_of(p * STEP, STEP), STEP)

    def hidden_product(p):
        right = w_all[:, :, :, columns(p)].reshape(512, STEP)
        out = jnp.dot(grad_t[...].reshape(512, 512), right, preferred_element_type=F32)
        return out.astype(BF16).reshape(2, 4, 64, STEP)

    def hidden_piece(p):
        out = hidden_product(p)
        for a in range(2):
            for b in range(4):
                xs[p, b, a * 64 : a * 64 + 64, :] = out[a, b]

    def weight_piece(p):
        right = hid_all[:, :, :, columns(p)].reshape(2, 256, STEP)
        out = jnp.dot(grad[0], right[0], preferred_element_type=F32)
        out += jnp.dot(grad[1], right[1], preferred_element_type=F32)
        ys[p] = out.astype(BF16).reshape(4, 128, STEP)

    def z_copy(i, d, *part):
        return pltpu.make_async_remote_copy(
            src_ref=z_send.at[(i, (z + d) % 8, *part)], dst_ref=z_recv.at[(i, z, *part)],
            send_sem=rz_s.at[i, d], recv_sem=rz_r.at[i, d], device_id=voc_peer(d, 0), device_id_type=MESH,
        )

    out = hidden_product(LAST)
    for a in range(2):
        for k in range(4):
            for b in range(4):
                zf_send[a * 4 + k, b] = out[a, b, k * 16 : k * 16 + 16]
    zf_copies = [
        send(zf_send.at[(z + d) % 8], zf_recv.at[z], zf_s.at[d], zf_r.at[d], voc_peer(d, 0)) for d in Z_ORDER[:-1]
    ]
    zf_recv[z] = zf_send[z]

    def x_pieces(i, work):
        work(2 * i, 0)
        pl.when(i < PAIRS - 1)(lambda: work(2 * i + 1, 1))

    def turn(i, _):
        @pl.when(i < PAIRS)
        def _():
            def product(p, h):
                hidden_piece(p)
                x_early(p, h)

            x_pieces(i, product)
            for h in range(2):
                weight_piece(2 * i + h)
                y_early(2 * i + h, h)

        @pl.when((i >= 1) & (i < PAIRS + 1))
        def _():
            x_pieces(i - 1, x_late)
            for h in range(2):
                y_late(2 * i - 2 + h, h)

        @pl.when(i >= 2)
        def _():
            pair = i - 2

            def total(p, h):
                z_send[pair, :, h] = x_total(p, h).astype(BF16).reshape(8, 16, STEP)

            x_pieces(pair, total)

            @pl.when(pair < PAIRS - 1)
            def _():
                for d in Z_ORDER[:-1]:
                    z_copy(pair, d).start()
                z_recv[pair, z, 1] = z_send[pair, z, 1]

            @pl.when(pair == PAIRS - 1)
            def _():
                for d in Z_ORDER[:-1]:
                    z_copy(pair, d, 0).start()

            z_recv[pair, z, 0] = z_send[pair, z, 0]
            for h in range(2):
                gw_ref[:, columns(2 * pair + h)] = y_total(2 * pair + h, h).astype(BF16)

        return 0

    lax.fori_loop(0, 3, turn, 0)
    arrive(zf_copies)
    out = zf_recv[0].astype(F32)
    for k in range(1, 8):
        out += zf_recv[k].astype(F32)
    xf_send[...] = out.astype(BF16)
    xf_copies = [
        send(xf_send.at[(x + d) % 4], xf_recv.at[x], xf_s.at[d], xf_r.at[d], x_peer(d)) for d in (2, 1, 3)
    ]
    xf_recv[x] = xf_send[x]
    lax.fori_loop(3, PAIRS + 2, turn, 0)
    arrive(cross_copies)
    c_z[z] = c_x[0] + c_x[1] + c_x[2] + c_x[3]
    cross_copies = to_z(c_z, cz_s, cz_r)

    def summed(i, h):
        out = z_recv[i, 0, h].astype(F32)
        for k in range(1, 8):
            out += z_recv[i, k, h].astype(F32)
        gh_ref[:, columns(2 * i + h)] = out.astype(BF16)

    arrive(xf_copies)
    gh_ref[:, LAST * STEP :] = sum(xf_recv[k].astype(F32) for k in range(4)).astype(BF16)

    def finish(i, _):
        @pl.when(i < PAIRS - 1)
        def _():
            for d in Z_ORDER[:-1]:
                z_copy(i, d).wait()
            summed(i, 1)

        @pl.when(i == PAIRS - 1)
        def _():
            for d in Z_ORDER[:-1]:
                z_copy(i, d, 0).wait()

        summed(i, 0)
        x_pieces(i, x_sent)
        for h in range(2):
            y_sent(2 * i + h, h)
        return 0

    lax.fori_loop(0, PAIRS, finish, 0)
    arrive(cross_copies)
    cross = sum(c_z[i][0:1] for i in range(8))
    kl = cross - norm_t + norm_d
    kl = jnp.where(x < 2, kl[:, :128], kl[:, 128:])
    kl_ref[...] = jnp.where(x % 2 == 0, kl, swap(kl))
    drain()


def body(hidden, head_weight, target_logits, vocab_order, draft_map, token_weight):
    tok = lax.axis_index("tok")
    ids = lax.dynamic_slice_in_dim(draft_map, tok * 8 * BLK, 8 * BLK, 0).reshape(8, BLK)
    ids = jnp.pad(ids, ((0, 0), (0, 128 - BLK)), constant_values=-2)
    order = jnp.pad(vocab_order, (0, 63 * 128 - COLS), constant_values=-1).reshape(63, 128)
    in_place = (target_logits.T, hidden.reshape(2, 64, D2), head_weight, token_weight.reshape(1, 128))

    vmem = pl.BlockSpec(memory_space=pltpu.VMEM)
    hbm = pl.BlockSpec(memory_space=pltpu.HBM)
    dma = pltpu.SemaphoreType.DMA
    scratch = [
        pltpu.VMEM((1, 128), F32),
        pltpu.VMEM((BLK, D2), BF16),
        pltpu.VMEM((COLS, 128), BF16),
        pltpu.VMEM((16, 8, 128), I32),
        pltpu.VMEM((128, 128), F32),
        pltpu.VMEM((128, 128), F32),
        pltpu.VMEM((8, 128), F32),
        pltpu.VMEM((8, 16, 128), BF16),
        pltpu.VMEM((16, 16, 128), BF16),
        pltpu.VMEM((8, 8, 256), I32),
        pltpu.SMEM((8, 8, 256), I32),
        pltpu.VMEM((COLS, 128), F32),
        pltpu.VMEM((8, 256, 128), F32),
        pltpu.VMEM((8, 2, 128, 128), BF16),
        pltpu.VMEM((16, 128, 128), BF16),
        pltpu.VMEM((16, 128), I32),
        pltpu.SMEM((16, 128), I32),
        pltpu.VMEM((4096, 128), F32),
        pltpu.VMEM((16, 128, 128), F32),
        pltpu.VMEM((4, 256, 128), BF16),
        pltpu.VMEM((4, 256, 128), BF16),
        pltpu.VMEM((512, 256), F32),
        pltpu.VMEM((2, 4, 64, D2), BF16),
        pltpu.VMEM((4, 2, 64, D2), BF16),
        pltpu.VMEM((512, 256), F32),
        pltpu.VMEM((512, 256), F32),
        pltpu.VMEM((512, 256), F32),
        pltpu.VMEM((4, 8, 256), F32),
        pltpu.VMEM((8, 8, 256), F32),
        pltpu.VMEM((2, 8, 128), F32),
        pltpu.VMEM((8, 8, 128), F32),
        pltpu.VMEM((4, 8, 128), F32),
        pltpu.VMEM((4, 8, 256), F32),
        pltpu.VMEM((8, 8, 256), F32),
        pltpu.VMEM((2, 512, 256), BF16),
        pltpu.VMEM((2, 4, 64, 512), BF16),
        pltpu.VMEM((2 * PAIRS, 4, 128, STEP), BF16),
        pltpu.VMEM((2 * PAIRS, 4, 128, STEP), BF16),
        pltpu.VMEM((2 * PAIRS, 128, STEP), BF16),
        pltpu.VMEM((2 * PAIRS, 128, STEP), BF16),
        pltpu.VMEM((2 * PAIRS, 2, 128, STEP), BF16),
        pltpu.VMEM((2 * PAIRS, 2, 128, STEP), BF16),
        pltpu.VMEM((PAIRS, 8, 2, 16, STEP), BF16),
        pltpu.VMEM((PAIRS, 8, 2, 16, STEP), BF16),
        pltpu.VMEM((8, 4, 16, STEP), BF16),
        pltpu.VMEM((8, 4, 16, STEP), BF16),
        pltpu.VMEM((4, 16, STEP), BF16),
        pltpu.VMEM((4, 16, STEP), BF16),
        dma((2, 16)),
        dma((12,)), dma((12,)),
        dma((5,)),
        dma((8,)),
        dma((16,)), dma((16,)),
        dma((16,)), dma((16,)),
        dma((4,)), dma((4,)),
        dma((2,)),
        dma((4,)), dma((4,)),
        dma((8,)), dma((8,)),
        dma((2,)),
        dma((8,)), dma((8,)),
        dma((4,)), dma((4,)),
        dma((4,)), dma((4,)),
        dma((8,)), dma((8,)),
        dma((2,)),
        dma((3, 2 * PAIRS)), dma((3, 2 * PAIRS)),
        dma((3, 2 * PAIRS)), dma((3, 2 * PAIRS)),
        dma((PAIRS, 8)), dma((PAIRS, 8)),
        dma((8,)), dma((8,)),
        dma((4,)), dma((4,)),
    ]
    kl, grad_hidden, grad_weight = pl.pallas_call(
        kernel,
        out_shape=(
            jax.ShapeDtypeStruct((1, 128), F32),
            jax.ShapeDtypeStruct((16, D2), BF16),
            jax.ShapeDtypeStruct((128, D2), BF16),
        ),
        in_specs=[vmem, vmem, hbm, hbm, hbm, hbm],
        out_specs=(vmem, vmem, vmem),
        scratch_shapes=scratch,
        compiler_params=pltpu.CompilerParams(
            collective_id=0, has_side_effects=True, vmem_limit_bytes=VMEM_LIMIT
        ),
        name="draft_head",
    )(ids, order, *(pltpu.with_memory_space_constraint(a, pltpu.HBM) for a in in_place))
    return kl[0, :64], grad_hidden, grad_weight[:BLK]


def solution(mesh):
    placed = (
        P("tok", "hid"),
        P(("tok", "voc"), "hid"),
        P("tok", ("voc", "hid")),
        P(("voc", "hid")),
        P(),
        P("tok"),
    )
    return jax.shard_map(
        body,
        mesh=mesh,
        in_specs=placed,
        out_specs=(P(("tok", "hid")), P(("tok", "voc"), "hid"), P(("tok", "voc"), "hid")),
        check_vma=False,
    )
```
